128 devices in a mesh: outer: 32 (over z, y, core), sw: 4 (over x).
Axes of the slice: x: 4, y: 4, z: 4, core: 2. Of those that a mesh axis runs over, the one named last changes fastest.
Arguments:
- path_state: bfloat16 [65536, 256], P(('outer', 'sw')), may hold values from -6 to 6
- link_state: bfloat16 [262144, 256], P(('outer', 'sw')), may hold values from -6 to 6
- hop_slot: int32 [65536, 8], P(('outer', 'sw')), may hold values from 0 to 1023
- hop_count: int32 [65536], P(('outer', 'sw')), may hold values from 2 to 8
- send_rows: int32 [16384, 8], P(('outer', 'sw')), may hold values from 0 to 2047
- w_input: bfloat16 [256, 768], replicated, may hold values from -0.375 to 0.375
- w_state: bfloat16 [256, 768], replicated, may hold values from -0.375 to 0.375
- w_agg: bfloat16 [256, 256], replicated, may hold values from -0.375 to 0.375
- path_cot: bfloat16 [65536, 256], P(('outer', 'sw')), may hold values from -6 to 6
- link_cot: bfloat16 [262144, 256], P(('outer', 'sw')), may hold values from -6 to 6
Outputs:
- grad_path: float32 [65536, 256], P(('outer', 'sw'))
- grad_link: float32 [262144, 256], P(('outer', 'sw'))
- grad_w_input: float32 [256, 768], replicated
- grad_w_state: float32 [256, 768], replicated
- grad_w_agg: float32 [256, 256], replicated
The draws below stay inside these ranges and needn't reach their ends.
Inputs may be any that keep to these rules, and one draw needn't show every extreme that they name: `hop_slot`: A slot s of a path on device q names row send_rows[(s // 8) * 128 + q, s % 8] of the links owned by device s // 8. `send_rows`: row q * 128 + d lists local link indices of device q sent to device d; an index may repeat.
All inputs are finite; a program needn't handle non-finite values.
Results may differ from the reference program's by a relative error of at most 0.0095.
Values may be sent and summed in bfloat16 or wider, within the bound.
No kernel may reach another device: no remote copies, remote signals or barrier semaphores. Data moves between devices by JAX's collectives and lax.ppermute only.
A program may use at most 192 MiB of HBM per device.

```python
import math
import jax
import jax.numpy as jnp
from jax import lax

H = 256
HOPS = 8
P_DEV = 512
L_DEV = 2048
CAP = 8
GATES = 768
PATHS = 65536
LINKS = 262144
N_OUTER = 32
N_SW = 4
DEVICES = 128


def set_ends(values, stream_key, smallest, largest):
    dims = values.shape
    place = [jax.random.randint(jax.random.fold_in(stream_key, axis), (), 0, dims[axis]) for axis in range(len(dims))]
    values = values.at[tuple(place)].set(smallest)
    longest = dims.index(max(dims))
    place[longest] = (place[longest] + 1) % dims[longest]
    return values.at[tuple(place)].set(largest)


def levels(stream_key, shape, pieces, least, largest):
    def one(axis_at, parts):
        draws = jax.random.uniform(jax.random.fold_in(jax.random.fold_in(stream_key, 6), axis_at), (parts,), jnp.float32, least / len(pieces), largest / len(pieces))
        return jnp.repeat(jnp.exp(draws), shape[axis_at] // parts).reshape((-1,) + (1,) * (len(shape) - axis_at - 1))

    loudness = one(*pieces[0])
    for cut in pieces[1:]:
        loudness = loudness * one(*cut)
    return loudness


def scatter_about(rng, extent, spread, limit, pieces=(), kind=jnp.bfloat16):
    result = spread * jax.random.normal(rng, extent, jnp.float32)
    if pieces:
        result = result * levels(rng, extent, pieces, -0.22, 0.18)
    return jnp.clip(result, -limit, limit).astype(kind)


def setup_inputs(seed: int = 0) -> dict:
    seeds = jax.random.split(jax.random.key(seed), 11)
    path_state = scatter_about(seeds[0], (PATHS, H), 1.0, 6.0, ((0, 128),))
    link_state = scatter_about(seeds[1], (LINKS, H), 1.0, 6.0, ((0, 128),))
    hop_slot = set_ends(jax.random.randint(seeds[2], (PATHS, HOPS), 0, DEVICES * CAP), jax.random.fold_in(seeds[2], 1), 0, (DEVICES * CAP) - 1).astype(jnp.int32)
    hop_count = set_ends(jax.random.randint(seeds[3], (PATHS,), 2, HOPS + 1), jax.random.fold_in(seeds[3], 1), 2, HOPS).astype(jnp.int32)
    send_rows = set_ends(jax.random.randint(seeds[4], (DEVICES * DEVICES, CAP), 0, L_DEV), jax.random.fold_in(seeds[4], 1), 0, L_DEV - 1).astype(jnp.int32)
    w_input = scatter_about(seeds[5], (H, GATES), H ** -0.5, 0.375)
    w_state = scatter_about(seeds[6], (H, GATES), H ** -0.5, 0.375)
    w_agg = scatter_about(seeds[7], (H, H), H ** -0.5, 0.375)
    path_cot = scatter_about(seeds[8], (PATHS, H), 1.0, 6.0, ((0, 128),))
    link_cot = scatter_about(seeds[9], (LINKS, H), 1.0, 6.0, ((0, 128),))
    return {"path_state": path_state, "link_state": link_state, "hop_slot": hop_slot, "hop_count": hop_count, "send_rows": send_rows, "w_input": w_input, "w_state": w_state, "w_agg": w_agg, "path_cot": path_cot, "link_cot": link_cot}


def gru_path(start_state, hop_inputs, hop_valid, input_weight, state_weight):
    width = start_state.shape[1]

    def hop_step(carried, hop_item):
        link_rows, keep_mask = hop_item
        from_input = jnp.dot(link_rows, input_weight.astype(jnp.bfloat16), preferred_element_type=jnp.float32)
        from_state = jnp.dot(carried.astype(jnp.bfloat16), state_weight.astype(jnp.bfloat16), preferred_element_type=jnp.float32)
        reset_gate = jax.nn.sigmoid(from_input[:, :width] + from_state[:, :width])
        update_gate = jax.nn.sigmoid(from_input[:, width:2 * width] + from_state[:, width:2 * width])
        candidate = jnp.tanh(from_input[:, 2 * width:] + reset_gate * from_state[:, 2 * width:])
        proposed = (1.0 - update_gate) * candidate + update_gate * carried
        keep_col = keep_mask[:, None]
        carried = keep_col * proposed + (1.0 - keep_col) * carried
        message = (keep_col * carried).astype(jnp.bfloat16)
        return (carried, message)
    return lax.scan(hop_step, start_state, (hop_inputs, hop_valid))

def link_backward(agg_round, w_agg, link_cot):
    preact = jnp.dot(agg_round, w_agg, preferred_element_type=jnp.float32)
    activated = jnp.tanh(preact)
    grad_pre = link_cot.astype(jnp.float32) * (1.0 - activated * activated)
    d_agg = jnp.dot(grad_pre, w_agg.astype(jnp.float32).T, precision=lax.Precision.HIGHEST).astype(jnp.bfloat16)
    wgrad = jnp.dot(agg_round.astype(jnp.float32).T, grad_pre, precision=lax.Precision.HIGHEST)
    return (link_cot.astype(jnp.float32), d_agg, wgrad)

def reference(path_state, link_state, hop_slot, hop_count, send_rows, w_input, w_state, w_agg, path_cot, link_cot):
    devices = N_OUTER * N_SW
    send_plan = send_rows.reshape(devices, devices, CAP)
    owner_dev = jnp.broadcast_to((jnp.arange(PATHS, dtype=jnp.int32) // P_DEV)[:, None], hop_slot.shape)
    source = hop_slot // CAP
    column = hop_slot % CAP
    link_ids = (source * L_DEV + send_plan[source, owner_dev, column]).astype(jnp.int32)
    hop_valid = (jnp.arange(HOPS, dtype=jnp.int32)[None, :] < hop_count[:, None]).astype(jnp.float32)
    block_links = link_ids.reshape(devices, P_DEV, HOPS).transpose(0, 2, 1)
    block_valid = hop_valid.reshape(devices, P_DEV, HOPS).transpose(0, 2, 1)
    block_start = path_state.reshape(devices, P_DEV, H)
    block_cot = path_cot.reshape(devices, P_DEV, H)
    input_f32 = w_input.astype(jnp.float32)
    state_f32 = w_state.astype(jnp.float32)

    def forward_block(aggregate, block):
        links_here, valid_here, start_here = block
        hop_inputs = link_state[links_here]
        _, messages = gru_path(start_here.astype(jnp.float32), hop_inputs, valid_here, input_f32, state_f32)
        aggregate = aggregate.at[links_here.reshape(-1)].add(messages.reshape(-1, H).astype(jnp.float32))
        return (aggregate, None)
    aggregate, _ = lax.scan(forward_block, jnp.zeros((LINKS, H), jnp.float32), (block_links, block_valid, block_start))
    link_grad, d_agg, wagg_grad = link_backward(aggregate.astype(jnp.bfloat16), w_agg, link_cot)

    def backward_block(carried, block):
        link_acc, input_acc, state_acc = carried
        links_here, valid_here, start_here, cot_here = block
        hop_inputs = link_state[links_here]

        def path_fn(start_state, inputs_here, input_weight, state_weight):
            return gru_path(start_state, inputs_here, valid_here, input_weight, state_weight)
        _, pullback = jax.vjp(path_fn, start_here.astype(jnp.float32), hop_inputs, input_f32, state_f32)
        d_start, d_inputs, d_input_w, d_state_w = pullback((cot_here.astype(jnp.float32), d_agg[links_here]))
        link_acc = link_acc.at[links_here.reshape(-1)].add(d_inputs.reshape(-1, H).astype(jnp.float32))
        return ((link_acc, input_acc + d_input_w, state_acc + d_state_w), d_start)
    zero_links = jnp.zeros((LINKS, H), jnp.float32)
    zero_gates = jnp.zeros((H, GATES), jnp.float32)
    totals, d_starts = lax.scan(backward_block, (zero_links, zero_gates, zero_gates), (block_links, block_valid, block_start, block_cot))
    link_acc, input_acc, state_acc = totals
    path_scale = 1.0 / math.sqrt(PATHS)
    link_scale = 1.0 / math.sqrt(LINKS)
    grad_path = d_starts.reshape(PATHS, H)
    grad_link = link_grad + link_acc
    return (grad_path, grad_link, input_acc * path_scale, state_acc * path_scale, wagg_grad * link_scale)
```

```python
import functools
import math

import jax
import jax.numpy as jnp
from jax import lax
from jax.experimental import pallas as pl
from jax.experimental.pallas import tpu as pltpu
from jax.sharding import PartitionSpec as P

F32 = jnp.float32
BF16 = jnp.bfloat16
AXES = ("outer", "sw")
VMEM_LIMIT = 56 * 1024 * 1024


def mm(a, b):
    return lax.dot_general(a, b, (((1,), (0,)), ((), ())), preferred_element_type=F32)


def mm_t(a, b):
    return lax.dot_general(a, b, (((1,), (1,)), ((), ())), preferred_element_type=F32)


def hot_rows(col, width):
    lanes = lax.broadcasted_iota(jnp.int32, (col.shape[0], width), 1)
    return jnp.where(col == lanes, 1.0, 0.0).astype(BF16)


def hot_cols(row, start, height):
    lines = lax.broadcasted_iota(jnp.int32, (height, row.shape[1]), 0) + start
    return jnp.where(row == lines, 1.0, 0.0).astype(BF16)


def call(kernel, outs, scratch, cost, *args):
    flops, moved = cost
    return pl.pallas_call(
        kernel,
        out_shape=outs,
        in_specs=[pl.BlockSpec(memory_space=pltpu.VMEM)] * len(args),
        out_specs=jax.tree.map(lambda _: pl.BlockSpec(memory_space=pltpu.VMEM), outs),
        scratch_shapes=scratch,
        compiler_params=pltpu.CompilerParams(vmem_limit_bytes=VMEM_LIMIT),
        cost_estimate=pl.CostEstimate(flops=flops, bytes_accessed=moved, transcendentals=0),
    )(*args)


def pick_kernel(rows_ref, link_ref, out_ref):
    links = link_ref.shape[0]
    tile = 256

    def body(i, carry):
        at = pl.ds(pl.multiple_of(i * tile, tile), tile)
        out_ref[at, :] = mm(hot_rows(rows_ref[at, :], links), link_ref[...]).astype(BF16)
        return carry

    lax.fori_loop(0, out_ref.shape[0] // tile, body, 0)


def halved(w_ref):
    width = w_ref.shape[0]
    lanes = lax.broadcasted_iota(jnp.int32, w_ref.shape, 1)
    w = w_ref[...].astype(F32)
    return jnp.where(lanes < 2 * width, 0.5 * w, w).astype(BF16)


def gates(a, b, width):
    r = 0.5 * jnp.tanh(a[:, :width] + b[:, :width]) + 0.5
    u = 0.5 * jnp.tanh(a[:, width : 2 * width] + b[:, width : 2 * width]) + 0.5
    bn = b[:, 2 * width :]
    n = jnp.tanh(a[:, 2 * width :] + r * bn)
    return r, u, n, bn


def forward_kernel(
    table_ref, col_ref, row_ref, start_ref, wi_ref, ws_ref,
    sums_ref, xs_ref, cs_ref, wi_s, ws_s, a_s, msg_s,
):
    hops, paths, width = xs_ref.shape
    slots = table_ref.shape[0]
    tile = 256
    wi_s[...] = halved(wi_ref)
    ws_s[...] = halved(ws_ref)

    for t in range(hops):
        for i in range(0, paths, tile):
            at = slice(i, i + tile)
            hot = hot_rows(col_ref[at, t : t + 1], slots)
            x = mm(hot, table_ref[...]).astype(BF16)
            xs_ref[t, at, :] = x
            a_s[t, at, :] = mm(x, wi_s[...])

    cs_ref[0] = start_ref[...].astype(F32)
    for t in range(hops):
        for i in range(0, paths, tile):
            at = slice(i, i + tile)
            c = cs_ref[t, at, :]
            b = mm(c.astype(BF16), ws_s[...])
            r, u, n, _ = gates(a_s[t, at, :], b, width)
            keep = col_ref[at, t : t + 1] >= 0
            c = jnp.where(keep, n + u * (c - n), c)
            if t + 1 < hops:
                cs_ref[t + 1, at, :] = c
            msg_s[t * paths + i : t * paths + i + tile, :] = c.astype(BF16)

    step = 256
    for i in range(0, slots, step):
        total = None
        for t in range(hops):
            hot = hot_cols(row_ref[t : t + 1, :], i, step)
            term = mm(hot, msg_s[t * paths : (t + 1) * paths, :])
            total = term if total is None else total + term
        sums_ref[i : i + step, :] = total.astype(BF16)


def factors_kernel(
    xs_ref, cs_ref, col_ref, wi_ref, ws_ref,
    fr_ref, fu_ref, fn_ref, fm_ref, fc_ref, xt_ref, ct_ref,
):
    t = pl.program_id(0)
    _, paths, width = xs_ref.shape
    wi = halved(wi_ref)
    ws = halved(ws_ref)
    tile = 256
    hop = lax.broadcasted_iota(jnp.int32, (1, col_ref.shape[1]), 1) == t
    for i in range(0, paths, tile):
        at = slice(i, i + tile)
        x = xs_ref[0, at, :]
        c = cs_ref[0, at, :]
        cb = c.astype(BF16)
        r, u, n, bn = gates(mm(x, wi), mm(cb, ws), width)
        slot = jnp.max(jnp.where(hop, col_ref[at, :], -1), axis=1, keepdims=True)
        keep = slot >= 0
        fn = jnp.where(keep, (1.0 - u) * (1.0 - n * n), 0.0)
        fm = fn * r
        fn_ref[0, at, :] = fn
        fm_ref[0, at, :] = fm
        fr_ref[0, at, :] = fm * bn * (1.0 - r)
        fu_ref[0, at, :] = jnp.where(keep, (c - n) * u * (1.0 - u), 0.0)
        fc_ref[0, at, :] = jnp.where(keep, u, 1.0)
        xt_ref[:, at] = x.astype(F32).T.astype(BF16)
        ct_ref[:, at] = c.T.astype(BF16)


def link_kernel(
    arrived_ref, row_ref, col_ref, w_ref, cot_ref, back_ref, agg_ref, pre_ref, d_s,
):
    links = cot_ref.shape[0]
    tile = 256

    def body(i, carry):
        start = pl.multiple_of(i * tile, tile)
        at = pl.ds(start, tile)
        agg = mm(hot_cols(row_ref[...], start, tile), arrived_ref[...]).astype(BF16)
        act = jnp.tanh(mm(agg, w_ref[...]))
        pre = cot_ref[at, :].astype(F32) * (1.0 - act * act)
        high = pre.astype(BF16)
        low = (pre - high.astype(F32)).astype(BF16)
        agg_ref[at, :] = agg
        pre_ref[at, :] = pre
        d_s[at, :] = (mm_t(high, w_ref[...]) + mm_t(low, w_ref[...])).astype(BF16)
        return carry

    lax.fori_loop(0, links // tile, body, 0)

    def pick(i, carry):
        at = pl.ds(pl.multiple_of(i * tile, tile), tile)
        back_ref[at, :] = mm(hot_rows(col_ref[at, :], links), d_s[...]).astype(BF16)
        return carry

    lax.fori_loop(0, back_ref.shape[0] // tile, pick, 0)


def link_grad_kernel(agg_ref, pre_ref, out_ref):
    links = agg_ref.shape[0]
    tile = 256
    out_ref[...] = jnp.zeros_like(out_ref)

    def body(i, carry):
        at = pl.ds(pl.multiple_of(i * tile, tile), tile)
        agg_t = agg_ref[at, :].astype(F32).T.astype(BF16)
        pre = pre_ref[at, :]
        high = pre.astype(BF16)
        low = (pre - high.astype(F32)).astype(BF16)
        out_ref[...] += mm(agg_t, high) + mm(agg_t, low)
        return carry

    lax.fori_loop(0, links // tile, body, 0)


def backward_kernel(
    table_ref, col_ref, row_ref, cot_ref, wi_ref, ws_ref,
    fr_ref, fu_ref, fn_ref, fm_ref, fc_ref, xt_ref, ct_ref,
    grad_ref, sums_ref, gi_ref, gs_ref, da_s, db_s, dx_s,
):
    step_id = pl.program_id(0)
    hops = pl.num_programs(0)
    t = hops - 1 - step_id
    paths, width = grad_ref.shape
    slots = table_ref.shape[0]
    tile = 256

    @pl.when(step_id == 0)
    def _():
        grad_ref[...] = cot_ref[...].astype(F32)
        gi_ref[...] = jnp.zeros_like(gi_ref)
        gs_ref[...] = jnp.zeros_like(gs_ref)

    hop = lax.broadcasted_iota(jnp.int32, (1, col_ref.shape[1]), 1) == t
    for i in range(0, paths, tile):
        at = slice(i, i + tile)
        slot = jnp.max(jnp.where(hop, col_ref[at, :], -1), axis=1, keepdims=True)
        d = grad_ref[at, :] + mm(hot_rows(slot, slots), table_ref[...])
        dr = (d * fr_ref[0, at, :]).astype(BF16)
        du = (d * fu_ref[0, at, :]).astype(BF16)
        dn = (d * fn_ref[0, at, :]).astype(BF16)
        dm = (d * fm_ref[0, at, :]).astype(BF16)
        da_s[at, :width] = dr
        da_s[at, width : 2 * width] = du
        da_s[at, 2 * width :] = dn
        db_s[at, :width] = dr
        db_s[at, width : 2 * width] = du
        db_s[at, 2 * width :] = dm
        back = mm_t(db_s[at, :], ws_ref[...]).astype(BF16).astype(F32)
        grad_ref[at, :] = d * fc_ref[0, at, :] + back
        dx = mm_t(da_s[at, :], wi_ref[...]).astype(BF16)
        dx_s[pl.ds(pl.multiple_of(t * paths + i, tile), tile), :] = dx
    gi_ref[...] += mm(xt_ref[...], da_s[...])
    gs_ref[...] += mm(ct_ref[...], db_s[...])

    @pl.when(step_id == hops - 1)
    def _():
        step = 256
        for i in range(0, slots, step):
            total = None
            for h in range(row_ref.shape[0]):
                hot = hot_cols(row_ref[h : h + 1, :], i, step)
                term = mm(hot, dx_s[h * paths : (h + 1) * paths, :])
                total = term if total is None else total + term
            sums_ref[i : i + step, :] = total.astype(BF16)


def share_kernel(parts_ref, out_ref):
    out_ref[...] = jnp.sum(parts_ref[...].astype(F32), axis=0)


def link_out_kernel(returned_ref, row_ref, cot_ref, out_ref):
    tile = 256

    def body(i, carry):
        start = pl.multiple_of(i * tile, tile)
        at = pl.ds(start, tile)
        total = mm(hot_cols(row_ref[...], start, tile), returned_ref[...])
        out_ref[at, :] = cot_ref[at, :].astype(F32) + total
        return carry

    lax.fori_loop(0, out_ref.shape[0] // tile, body, 0)


def exchange(rows):
    return lax.all_to_all(rows, AXES, split_axis=0, concat_axis=0, tiled=True)


def per_device(
    path_state, link_state, hop_slot, hop_count, send_rows,
    w_input, w_state, w_agg, path_cot, link_cot,
):
    devices = lax.axis_size("outer") * lax.axis_size("sw")
    paths, width = path_state.shape
    hops = hop_slot.shape[1]
    links = link_state.shape[0]
    capacity = send_rows.shape[1]
    slots = devices * capacity
    gate_cols = w_input.shape[1]
    shape = jax.ShapeDtypeStruct

    send_row = send_rows.reshape(1, slots)
    send_col = send_rows.reshape(slots, 1)
    rows = call(
        pick_kernel, shape((slots, width), BF16), [],
        (2 * slots * links * width, 2 * links * width), send_col, link_state,
    )
    table = exchange(rows.reshape(devices, capacity, width)).reshape(slots, width)

    valid = jnp.arange(hops, dtype=jnp.int32)[None, :] < hop_count[:, None]
    slot_col = jnp.where(valid, hop_slot, -1)
    slot_row = jnp.where(valid.T, hop_slot.T, -1)
    sums, xs, cs = call(
        forward_kernel,
        (
            shape((slots, width), BF16),
            shape((hops, paths, width), BF16),
            shape((hops, paths, width), F32),
        ),
        [
            pltpu.VMEM((width, gate_cols), BF16),
            pltpu.VMEM((width, gate_cols), BF16),
            pltpu.VMEM((hops, paths, gate_cols), F32),
            pltpu.VMEM((hops * paths, width), BF16),
        ],
        (4 * hops * paths * slots * width, 8 * hops * paths * width),
        table, slot_col, slot_row, path_state, w_input, w_state,
    )
    arrived = exchange(sums.reshape(devices, capacity, width)).reshape(slots, width)

    whole = lambda *dims: pl.BlockSpec(dims, lambda i: (0,) * len(dims))
    factor = shape((hops, paths, width), F32)
    turned = shape((width, hops * paths), BF16)
    hop_block = pl.BlockSpec((1, paths, width), lambda i: (i, 0, 0))
    turned_block = pl.BlockSpec((width, paths), lambda i: (0, i))
    factors = pl.pallas_call(
        factors_kernel,
        grid=(hops,),
        out_shape=(factor,) * 5 + (turned,) * 2,
        in_specs=[
            hop_block, hop_block, whole(paths, hops),
            whole(width, gate_cols), whole(width, gate_cols),
        ],
        out_specs=(hop_block,) * 5 + (turned_block,) * 2,
        compiler_params=pltpu.CompilerParams(vmem_limit_bytes=VMEM_LIMIT),
        cost_estimate=pl.CostEstimate(
            flops=4 * hops * paths * width * gate_cols,
            bytes_accessed=32 * hops * paths * width, transcendentals=0,
        ),
    )(xs, cs, slot_col, w_input, w_state)

    back, agg, pre = call(
        link_kernel,
        (shape((slots, width), BF16), shape((links, width), BF16), shape((links, width), F32)),
        [pltpu.VMEM((links, width), BF16)],
        (4 * slots * links * width, 8 * links * width),
        arrived, send_row, send_col, w_agg, link_cot,
    )
    back_table = exchange(back.reshape(devices, capacity, width)).reshape(slots, width)
    agg_grad = call(
        link_grad_kernel, shape((width, width), F32), [],
        (4 * links * width * width, 6 * links * width), agg, pre,
    )

    last = hops - 1
    hop_back = pl.BlockSpec((1, paths, width), lambda i: (last - i, 0, 0))
    turned_back = pl.BlockSpec((width, paths), lambda i: (0, last - i))
    grad_path, input_sums, input_grad, state_grad = pl.pallas_call(
        backward_kernel,
        grid=(hops,),
        out_shape=(
            shape((paths, width), F32),
            shape((slots, width), BF16),
            shape((width, gate_cols), F32),
            shape((width, gate_cols), F32),
        ),
        in_specs=[
            whole(slots, width), whole(paths, hops), whole(hops, paths), whole(paths, width),
            whole(width, gate_cols), whole(width, gate_cols),
        ] + [hop_back] * 5 + [turned_back] * 2,
        out_specs=(
            whole(paths, width), whole(slots, width),
            whole(width, gate_cols), whole(width, gate_cols),
        ),
        scratch_shapes=[
            pltpu.VMEM((paths, gate_cols), BF16),
            pltpu.VMEM((paths, gate_cols), BF16),
            pltpu.VMEM((hops * paths, width), BF16),
        ],
        compiler_params=pltpu.CompilerParams(vmem_limit_bytes=VMEM_LIMIT),
        cost_estimate=pl.CostEstimate(
            flops=12 * hops * paths * width * gate_cols,
            bytes_accessed=32 * hops * paths * width, transcendentals=0,
        ),
    )(back_table, slot_col, slot_row, path_cot, w_input, w_state, *factors)

    grads = jnp.concatenate(
        [
            input_grad.reshape(-1, width), state_grad.reshape(-1, width), agg_grad,
        ],
        axis=0,
    ).astype(BF16)
    share = grads.shape[0] // devices
    both = jnp.concatenate(
        [input_sums.reshape(devices, capacity, width), grads.reshape(devices, share, width)],
        axis=1,
    )
    got = exchange(both)
    returned = got[:, :capacity].reshape(slots, width)
    mine = call(
        share_kernel, shape((share, width), F32), [],
        (devices * share * width, 2 * devices * share * width), got[:, capacity:],
    )
    spread = jnp.broadcast_to(mine.astype(BF16)[None], (devices, share, width))
    total = exchange(spread).reshape(devices * share, width).astype(F32)
    grad_link = call(
        link_out_kernel, shape((links, width), F32), [],
        (2 * slots * links * width, 6 * links * width), returned, send_row, link_cot,
    )
    span = width * gate_cols // width
    path_scale = 1.0 / math.sqrt(paths * devices)
    link_scale = 1.0 / math.sqrt(links * devices)
    return (
        grad_path,
        grad_link,
        total[:span].reshape(width, gate_cols) * path_scale,
        total[span : 2 * span].reshape(width, gate_cols) * path_scale,
        total[2 * span :] * link_scale,
    )


def solution(mesh):
    split = P(AXES, None)
    return jax.shard_map(
        per_device,
        mesh=mesh,
        in_specs=(split, split, split, P(AXES), split, P(), P(), P(), split, split),
        out_specs=(split, split, P(), P(), P()),
        check_vma=False,
    )
```

```python
import functools
import math

import jax
import jax.numpy as jnp
from jax import lax
from jax.experimental import pallas as pl
from jax.experimental.pallas import tpu as pltpu
from jax.sharding import PartitionSpec as P

F32 = jnp.float32
BF16 = jnp.bfloat16
AXES = ("outer", "sw")
VMEM_LIMIT = 56 * 1024 * 1024


def mm(a, b):
    return lax.dot_general(a, b, (((1,), (0,)), ((), ())), preferred_element_type=F32)


def mm_t(a, b):
    return lax.dot_general(a, b, (((1,), (1,)), ((), ())), preferred_element_type=F32)


def hot_rows(col, width):
    lanes = lax.broadcasted_iota(jnp.int32, (col.shape[0], width), 1)
    return jnp.where(col == lanes, 1.0, 0.0).astype(BF16)


def hot_cols(row, start, height):
    lines = lax.broadcasted_iota(jnp.int32, (height, row.shape[1]), 0) + start
    return jnp.where(row == lines, 1.0, 0.0).astype(BF16)


VMEM = pl.BlockSpec(memory_space=pltpu.VMEM)
ANY = pl.BlockSpec(memory_space=pl.ANY)


def call(kernel, outs, scratch, cost, *args, in_specs=None, out_specs=None):
    flops, moved = cost
    return pl.pallas_call(
        kernel,
        out_shape=outs,
        in_specs=in_specs or [VMEM] * len(args),
        out_specs=out_specs or jax.tree.map(lambda _: VMEM, outs),
        scratch_shapes=scratch,
        compiler_params=pltpu.CompilerParams(vmem_limit_bytes=VMEM_LIMIT),
        cost_estimate=pl.CostEstimate(flops=flops, bytes_accessed=moved, transcendentals=0),
    )(*args)


def pick_kernel(rows_ref, link_ref, out_ref):
    links = link_ref.shape[0]
    tile = 256

    def body(i, carry):
        at = pl.ds(pl.multiple_of(i * tile, tile), tile)
        out_ref[at, :] = mm(hot_rows(rows_ref[at, :], links), link_ref[...]).astype(BF16)
        return carry

    lax.fori_loop(0, out_ref.shape[0] // tile, body, 0)


def halved(w_ref):
    width = w_ref.shape[0]
    lanes = lax.broadcasted_iota(jnp.int32, w_ref.shape, 1)
    w = w_ref[...].astype(F32)
    return jnp.where(lanes < 2 * width, 0.5 * w, w).astype(BF16)


def gates(a, b, width):
    r = 0.5 * jnp.tanh(a[:, :width] + b[:, :width]) + 0.5
    u = 0.5 * jnp.tanh(a[:, width : 2 * width] + b[:, width : 2 * width]) + 0.5
    bn = b[:, 2 * width :]
    n = jnp.tanh(a[:, 2 * width :] + r * bn)
    return r, u, n, bn


def forward_kernel(
    table_ref, col_ref, row_ref, start_ref, wi_ref, ws_ref,
    sums_ref, xs_ref, cs_ref, wi_s, ws_s, a_s, x_s, c_s, msg_s, sem,
):
    hops, paths, width = x_s.shape
    slots = table_ref.shape[0]
    tile = 256
    wi_s[...] = halved(wi_ref)
    ws_s[...] = halved(ws_ref)

    def saves(t):
        return (
            pltpu.make_async_copy(x_s.at[t], xs_ref.at[t], sem.at[0, t]),
            pltpu.make_async_copy(c_s.at[t], cs_ref.at[t], sem.at[1, t]),
        )

    def enter(t, i):
        at = slice(i, i + tile)
        x = mm(hot_rows(col_ref[at, t : t + 1], slots), table_ref[...]).astype(BF16)
        x_s[t, at, :] = x
        a_s[t, at, :] = mm(x, wi_s[...])

    c_s[0] = start_ref[...].astype(F32)
    for i in range(0, paths, tile):
        enter(0, i)
    for t in range(hops):
        for i in range(0, paths, tile):
            at = slice(i, i + tile)
            if t + 1 < hops:
                enter(t + 1, i)
            c = c_s[t, at, :]
            b = mm(c.astype(BF16), ws_s[...])
            r, u, n, _ = gates(a_s[t, at, :], b, width)
            keep = col_ref[at, t : t + 1] >= 0
            c = jnp.where(keep, n + u * (c - n), c)
            if t + 1 < hops:
                c_s[t + 1, at, :] = c
            msg_s[t * paths + i : t * paths + i + tile, :] = c.astype(BF16)
    for t in range(hops):
        for copy in saves(t):
            copy.start()

    step = 256
    for i in range(0, slots, step):
        total = None
        for t in range(hops):
            hot = hot_cols(row_ref[t : t + 1, :], i, step)
            term = mm(hot, msg_s[t * paths : (t + 1) * paths, :])
            total = term if total is None else total + term
        sums_ref[i : i + step, :] = total.astype(BF16)
    for t in range(hops):
        for copy in saves(t):
            copy.wait()


def factors_kernel(
    xs_ref, cs_ref, col_ref, wi_ref, ws_ref,
    fr_ref, fu_ref, fn_ref, fm_ref, fc_ref, xt_ref, ct_ref,
):
    t = pl.program_id(0)
    _, paths, width = xs_ref.shape
    wi = halved(wi_ref)
    ws = halved(ws_ref)
    tile = 256
    hop = lax.broadcasted_iota(jnp.int32, (1, col_ref.shape[1]), 1) == t
    for i in range(0, paths, tile):
        at = slice(i, i + tile)
        x = xs_ref[0, at, :]
        c = cs_ref[0, at, :]
        cb = c.astype(BF16)
        r, u, n, bn = gates(mm(x, wi), mm(cb, ws), width)
        slot = jnp.max(jnp.where(hop, col_ref[at, :], -1), axis=1, keepdims=True)
        keep = slot >= 0
        fn = jnp.where(keep, (1.0 - u) * (1.0 - n * n), 0.0)
        fm = fn * r
        fn_ref[0, at, :] = fn
        fm_ref[0, at, :] = fm
        fr_ref[0, at, :] = fm * bn * (1.0 - r)
        fu_ref[0, at, :] = jnp.where(keep, (c - n) * u * (1.0 - u), 0.0)
        fc_ref[0, at, :] = jnp.where(keep, u, 1.0)
        xt_ref[:, at] = x.astype(F32).T.astype(BF16)
        ct_ref[:, at] = c.T.astype(BF16)


def link_tile(arrived_ref, row_ref, w_ref, cot_ref, start, tile):
    at = pl.ds(start, tile)
    agg = mm(hot_cols(row_ref[...], start, tile), arrived_ref[...]).astype(BF16)
    act = jnp.tanh(mm(agg, w_ref[...]))
    pre = cot_ref[at, :].astype(F32) * (1.0 - act * act)
    high = pre.astype(BF16)
    low = (pre - high.astype(F32)).astype(BF16)
    return agg, high, low


def link_kernel(arrived_ref, row_ref, col_ref, w_ref, cot_ref, back_ref, d_s):
    links = cot_ref.shape[0]
    tile = 256
    for i in range(0, links, tile):
        _, high, low = link_tile(arrived_ref, row_ref, w_ref, cot_ref, i, tile)
        d_s[i : i + tile, :] = (mm_t(high, w_ref[...]) + mm_t(low, w_ref[...])).astype(BF16)
    for i in range(0, back_ref.shape[0], tile):
        at = slice(i, i + tile)
        back_ref[at, :] = mm(hot_rows(col_ref[at, :], links), d_s[...]).astype(BF16)


def link_grad_kernel(arrived_ref, row_ref, w_ref, cot_ref, out_ref):
    tile = 256
    out_ref[...] = jnp.zeros_like(out_ref)

    def body(i, carry):
        start = pl.multiple_of(i * tile, tile)
        agg, high, low = link_tile(arrived_ref, row_ref, w_ref, cot_ref, start, tile)
        agg_t = agg.astype(F32).T.astype(BF16)
        out_ref[...] += mm(agg_t, high) + mm(agg_t, low)
        return carry

    lax.fori_loop(0, cot_ref.shape[0] // tile, body, 0)


def backward_kernel(
    table_ref, col_ref, cot_ref, wi_ref, ws_ref, agg_grad_ref,
    fr_ref, fu_ref, fn_ref, fm_ref, fc_ref, xt_ref, ct_ref,
    grad_ref, da_ref, grads_ref,
    f_s, xt_s, ct_s, m_s, da_s, db_s, gi_s, gs_s, sem, da_sem,
):
    _, hops, paths, width = f_s.shape
    slots = table_ref.shape[0]
    tile = 256

    def loads(t):
        at = pl.ds(t * paths, paths)
        pairs = [(ref.at[t], f_s.at[k, t]) for k, ref in enumerate(
            (fr_ref, fu_ref, fn_ref, fm_ref, fc_ref))]
        pairs += [(xt_ref.at[:, at], xt_s.at[:, at]), (ct_ref.at[:, at], ct_s.at[:, at])]
        return [
            pltpu.make_async_copy(source, target, sem.at[k, t])
            for k, (source, target) in enumerate(pairs)
        ]

    def save(t):
        return pltpu.make_async_copy(da_s.at[t], da_ref.at[t], da_sem.at[t])

    order = list(range(hops))[::-1]
    for t in order:
        for copy in loads(t):
            copy.start()

    grad_ref[...] = cot_ref[...].astype(F32)

    def fetch(t, i):
        at = slice(i, i + tile)
        m_s[t, at, :] = mm(hot_rows(col_ref[at, t : t + 1], slots), table_ref[...])

    def weigh(t):
        at = slice(t * paths, (t + 1) * paths)
        gi = mm(xt_s[:, at], da_s[t])
        gs = mm(ct_s[:, at], db_s[t])
        if t == hops - 1:
            gi_s[...] = gi
            gs_s[...] = gs
        else:
            gi_s[...] += gi
            gs_s[...] += gs

    for i in range(0, paths, tile):
        fetch(hops - 1, i)
    for t in order:
        for copy in loads(t):
            copy.wait()
        for i in range(0, paths, tile):
            at = slice(i, i + tile)
            if t > 0:
                fetch(t - 1, i)
            d = grad_ref[at, :] + m_s[t, at, :]
            dr = (d * f_s[0, t, at, :]).astype(BF16)
            du = (d * f_s[1, t, at, :]).astype(BF16)
            da_s[t, at, :width] = dr
            da_s[t, at, width : 2 * width] = du
            da_s[t, at, 2 * width :] = (d * f_s[2, t, at, :]).astype(BF16)
            db_s[t, at, :width] = dr
            db_s[t, at, width : 2 * width] = du
            db_s[t, at, 2 * width :] = (d * f_s[3, t, at, :]).astype(BF16)
            back = mm_t(db_s[t, at, :], ws_ref[...]).astype(BF16).astype(F32)
            grad_ref[at, :] = d * f_s[4, t, at, :] + back
        if t < hops - 1:
            weigh(t + 1)
    for t in order:
        save(t).start()
    weigh(0)
    for k in range(3):
        part = slice(k * width, (k + 1) * width)
        grads_ref[part, :] = gi_s[:, part].astype(BF16)
        grads_ref[3 * width + k * width : 3 * width + (k + 1) * width, :] = gs_s[:, part].astype(BF16)
    grads_ref[6 * width : 7 * width, :] = agg_grad_ref[...].astype(BF16)
    grads_ref[7 * width :, :] = jnp.zeros_like(agg_grad_ref).astype(BF16)
    for t in order:
        save(t).wait()


def input_kernel(da_ref, row_ref, wi_ref, sums_ref, dx_s):
    hops, paths, _ = da_ref.shape
    slots = sums_ref.shape[0]
    for t in range(hops):
        dx_s[t * paths : (t + 1) * paths, :] = mm_t(da_ref[t], wi_ref[...]).astype(BF16)
    step = 256
    for i in range(0, slots, step):
        total = None
        for t in range(hops):
            hot = hot_cols(row_ref[t : t + 1, :], i, step)
            term = mm(hot, dx_s[t * paths : (t + 1) * paths, :])
            total = term if total is None else total + term
        sums_ref[i : i + step, :] = total.astype(BF16)


def share_kernel(parts_ref, out_ref):
    total = jnp.sum(parts_ref[...].astype(F32), axis=0).astype(BF16)
    out_ref[...] = jnp.broadcast_to(total[None], out_ref.shape)


def link_out_kernel(returned_ref, row_ref, cot_ref, out_ref):
    tile = 256
    for i in range(0, out_ref.shape[0], tile):
        at = slice(i, i + tile)
        total = mm(hot_cols(row_ref[...], i, tile), returned_ref[...])
        out_ref[at, :] = cot_ref[at, :].astype(F32) + total


def final_kernel(path_scale, link_scale, total_ref, gi_ref, gs_ref, ga_ref):
    width = ga_ref.shape[0]
    for k in range(3):
        part = slice(k * width, (k + 1) * width)
        other = slice((k + 3) * width, (k + 4) * width)
        gi_ref[:, part] = total_ref[part, :].astype(F32) * path_scale
        gs_ref[:, part] = total_ref[other, :].astype(F32) * path_scale
    ga_ref[...] = total_ref[6 * width : 7 * width, :].astype(F32) * link_scale


def exchange(rows):
    return lax.all_to_all(rows, AXES, split_axis=0, concat_axis=0, tiled=True)


def per_device(
    path_state, link_state, hop_slot, hop_count, send_rows,
    w_input, w_state, w_agg, path_cot, link_cot,
):
    devices = lax.axis_size("outer") * lax.axis_size("sw")
    paths, width = path_state.shape
    hops = hop_slot.shape[1]
    links = link_state.shape[0]
    capacity = send_rows.shape[1]
    slots = devices * capacity
    gate_cols = w_input.shape[1]
    shape = jax.ShapeDtypeStruct

    send_row = send_rows.reshape(1, slots)
    send_col = send_rows.reshape(slots, 1)
    rows = call(
        pick_kernel, shape((slots, width), BF16), [],
        (2 * slots * links * width, 2 * links * width), send_col, link_state,
    )
    table = exchange(rows.reshape(devices, capacity, width)).reshape(slots, width)

    valid = jnp.arange(hops, dtype=jnp.int32)[None, :] < hop_count[:, None]
    slot_col = jnp.where(valid, hop_slot, -1)
    slot_row = jnp.where(valid.T, hop_slot.T, -1)
    sums, xs, cs = call(
        forward_kernel,
        (
            shape((slots, width), BF16),
            shape((hops, paths, width), BF16),
            shape((hops, paths, width), F32),
        ),
        [
            pltpu.VMEM((width, gate_cols), BF16),
            pltpu.VMEM((width, gate_cols), BF16),
            pltpu.VMEM((hops, paths, gate_cols), F32),
            pltpu.VMEM((hops, paths, width), BF16),
            pltpu.VMEM((hops, paths, width), F32),
            pltpu.VMEM((hops * paths, width), BF16),
            pltpu.SemaphoreType.DMA((2, hops)),
        ],
        (4 * hops * paths * slots * width, 8 * hops * paths * width),
        table, slot_col, slot_row, path_state, w_input, w_state,
        out_specs=(VMEM, ANY, ANY),
    )
    arrived = exchange(sums.reshape(devices, capacity, width)).reshape(slots, width)

    whole = lambda *dims: pl.BlockSpec(dims, lambda i: (0,) * len(dims))
    factor = shape((hops, paths, width), F32)
    turned = shape((width, hops * paths), BF16)
    hop_block = pl.BlockSpec((1, paths, width), lambda i: (i, 0, 0))
    turned_block = pl.BlockSpec((width, paths), lambda i: (0, i))
    factors = pl.pallas_call(
        factors_kernel,
        grid=(hops,),
        out_shape=(factor,) * 5 + (turned,) * 2,
        in_specs=[
            hop_block, hop_block, whole(paths, hops),
            whole(width, gate_cols), whole(width, gate_cols),
        ],
        out_specs=(hop_block,) * 5 + (turned_block,) * 2,
        compiler_params=pltpu.CompilerParams(vmem_limit_bytes=VMEM_LIMIT),
        cost_estimate=pl.CostEstimate(
            flops=4 * hops * paths * width * gate_cols,
            bytes_accessed=32 * hops * paths * width, transcendentals=0,
        ),
    )(xs, cs, slot_col, w_input, w_state)
    arrived, factors = lax.optimization_barrier((arrived, factors))

    back = call(
        link_kernel, shape((slots, width), BF16), [pltpu.VMEM((links, width), BF16)],
        (4 * slots * links * width, 8 * links * width),
        arrived, send_row, send_col, w_agg, link_cot,
    )
    back_table = exchange(back.reshape(devices, capacity, width)).reshape(slots, width)
    agg_grad = call(
        link_grad_kernel, shape((width, width), F32), [],
        (4 * links * width * width, 6 * links * width), arrived, send_row, w_agg, link_cot,
    )
    back_table, agg_grad = lax.optimization_barrier((back_table, agg_grad))

    grad_path, da, grads = call(
        backward_kernel,
        (
            shape((paths, width), F32),
            shape((hops, paths, gate_cols), BF16),
            shape((8 * width, width), BF16),
        ),
        [
            pltpu.VMEM((5, hops, paths, width), F32),
            pltpu.VMEM((width, hops * paths), BF16),
            pltpu.VMEM((width, hops * paths), BF16),
            pltpu.VMEM((hops, paths, width), F32),
            pltpu.VMEM((hops, paths, gate_cols), BF16),
            pltpu.VMEM((hops, paths, gate_cols), BF16),
            pltpu.VMEM((width, gate_cols), F32),
            pltpu.VMEM((width, gate_cols), F32),
            pltpu.SemaphoreType.DMA((7, hops)),
            pltpu.SemaphoreType.DMA((hops,)),
        ],
        (10 * hops * paths * width * gate_cols, 32 * hops * paths * width),
        back_table, slot_col, path_cot, w_input, w_state, agg_grad, *factors,
        in_specs=[VMEM] * 6 + [ANY] * 7,
        out_specs=(VMEM, ANY, VMEM),
    )
    share = grads.shape[0] // devices
    parts = exchange(grads.reshape(devices, share, width))
    input_sums = call(
        input_kernel, shape((slots, width), BF16), [pltpu.VMEM((hops * paths, width), BF16)],
        (2 * hops * paths * (gate_cols + slots) * width, 2 * hops * paths * gate_cols),
        da, slot_row, w_input,
    )
    returned = exchange(input_sums.reshape(devices, capacity, width)).reshape(slots, width)
    mine = call(
        share_kernel, shape((devices, share, width), BF16), [],
        (devices * share * width, 4 * devices * share * width), parts,
    )
    total = exchange(mine).reshape(devices * share, width)
    grad_link = call(
        link_out_kernel, shape((links, width), F32), [],
        (2 * slots * links * width, 6 * links * width), returned, send_row, link_cot,
    )
    path_scale = 1.0 / math.sqrt(paths * devices)
    link_scale = 1.0 / math.sqrt(links * devices)
    wide = shape((width, gate_cols), F32)
    input_grad, state_grad, agg_total = call(
        functools.partial(final_kernel, path_scale, link_scale),
        (wide, wide, shape((width, width), F32)), [],
        (8 * width * width, 40 * width * width), total,
    )
    return grad_path, grad_link, input_grad, state_grad, agg_total


def solution(mesh):
    split = P(AXES, None)
    return jax.shard_map(
        per_device,
        mesh=mesh,
        in_specs=(split, split, split, P(AXES), split, P(), P(), P(), split, split),
        out_specs=(split, split, P(), P(), P()),
        check_vma=False,
    )
```

```python
import functools
import math

import jax
import jax.numpy as jnp
from jax import lax
from jax.experimental import pallas as pl
from jax.experimental.pallas import tpu as pltpu
from jax.sharding import PartitionSpec as P

F32 = jnp.float32
BF16 = jnp.bfloat16
AXES = ("outer", "sw")
MIB = 1024 * 1024
VMEM = pl.BlockSpec(memory_space=pltpu.VMEM)
ANY = pl.BlockSpec(memory_space=pl.ANY)


def mm(a, b):
    return lax.dot_general(a, b, (((1,), (0,)), ((), ())), preferred_element_type=F32)


def mm_t(a, b):
    return lax.dot_general(a, b, (((1,), (1,)), ((), ())), preferred_element_type=F32)


def t_mm(a, b):
    return lax.dot_general(a, b, (((0,), (0,)), ((), ())), preferred_element_type=F32)


def hot_cols(row, start, height):
    lines = lax.broadcasted_iota(jnp.int32, (height, row.shape[1]), 0) + start
    return jnp.where(row == lines, 1.0, 0.0).astype(BF16)


def call(kernel, outs, scratch, cost, *args, in_specs=None, out_specs=None):
    flops, moved, room = cost
    return pl.pallas_call(
        kernel,
        out_shape=outs,
        in_specs=in_specs or [VMEM] * len(args),
        out_specs=out_specs or jax.tree.map(lambda _: VMEM, outs),
        scratch_shapes=scratch,
        compiler_params=pltpu.CompilerParams(vmem_limit_bytes=room * MIB),
        cost_estimate=pl.CostEstimate(flops=flops, bytes_accessed=moved, transcendentals=0),
    )(*args)


def pick_kernel(turned_ref, link_ref, out_ref, row_ref):
    capacity, devices = turned_ref.shape
    slots = capacity * devices
    links = link_ref.shape[0]
    listed = turned_ref[...]
    high = (listed >> 8).astype(F32).astype(BF16)
    low = (listed & 255).astype(F32).astype(BF16)
    owner = lax.broadcasted_iota(jnp.int32, (devices, slots), 0)
    place = lax.broadcasted_iota(jnp.int32, (devices, slots), 1)
    spread = jnp.where(place // capacity == owner, 1.0, 0.0).astype(BF16)
    wide = mm(high, spread) * 256.0 + mm(low, spread)
    line = lax.broadcasted_iota(jnp.int32, (capacity, slots), 0)
    at = lax.broadcasted_iota(jnp.int32, (capacity, slots), 1)
    row = jnp.sum(jnp.where(at % capacity == line, wide, 0.0), axis=0, keepdims=True)
    row_ref[...] = row.astype(jnp.int32)
    step = 512
    total = None
    for i in range(0, links, step):
        term = t_mm(hot_cols(row_ref[...], i, step), link_ref[i : i + step, :])
        total = term if total is None else total + term
    out_ref[...] = total.astype(BF16)


def pick_again_kernel(row_ref, link_ref, out_ref):
    step = 512
    total = None
    for i in range(0, link_ref.shape[0], step):
        term = t_mm(hot_cols(row_ref[...], i, step), link_ref[i : i + step, :])
        total = term if total is None else total + term
    out_ref[...] = total.astype(BF16)


def halved(w_ref):
    width = w_ref.shape[0]
    lanes = lax.broadcasted_iota(jnp.int32, w_ref.shape, 1)
    w = w_ref[...].astype(F32)
    return jnp.where(lanes < 2 * width, 0.5 * w, w).astype(BF16)


def gates(a, b, width):
    r = 0.5 * jnp.tanh(a[:, :width] + b[:, :width]) + 0.5
    u = 0.5 * jnp.tanh(a[:, width : 2 * width] + b[:, width : 2 * width]) + 0.5
    bn = b[:, 2 * width :]
    n = jnp.tanh(a[:, 2 * width :] + r * bn)
    return r, u, n, bn


def forward_kernel(
    table_ref, count_ref, row_ref, start_ref, wi_ref, ws_ref,
    sums_ref, xs_ref, cs_ref, table_s, wi_s, ws_s, a_s, x_s, c_s, msg_s, sem, table_sem,
):
    hops, paths, width = x_s.shape
    slots = table_ref.shape[0]
    tile = 256
    arrival = pltpu.make_async_copy(table_ref, table_s, table_sem)
    arrival.start()
    wi_s[...] = halved(wi_ref)
    ws_s[...] = halved(ws_ref)
    c_s[0] = start_ref[...].astype(F32)
    arrival.wait()

    def saves(t):
        return (
            pltpu.make_async_copy(x_s.at[t], xs_ref.at[t], sem.at[0, t]),
            pltpu.make_async_copy(c_s.at[t], cs_ref.at[t], sem.at[1, t]),
        )

    def enter(t, i):
        at = slice(i, i + tile)
        hot = hot_cols(row_ref[t : t + 1, at], 0, slots)
        x = t_mm(hot, table_s[...]).astype(BF16)
        x_s[t, at, :] = x
        a_s[t, at, :] = mm(x, wi_s[...])

    for i in range(0, paths, tile):
        enter(0, i)
    for t in range(hops):
        for i in range(0, paths, tile):
            at = slice(i, i + tile)
            if t + 1 < hops:
                enter(t + 1, i)
            c = c_s[t, at, :]
            b = mm(c.astype(BF16), ws_s[...])
            r, u, n, _ = gates(a_s[t, at, :], b, width)
            c = jnp.where(count_ref[at, :] > t, n + u * (c - n), c)
            if t + 1 < hops:
                c_s[t + 1, at, :] = c
            msg_s[t * paths + i : t * paths + i + tile, :] = c.astype(BF16)
    for t in range(hops):
        for copy in saves(t):
            copy.start()

    add_up(row_ref, msg_s, sums_ref)
    for t in range(hops):
        for copy in saves(t):
            copy.wait()


def add_up(row_ref, values, sums_ref):
    hops, paths = row_ref.shape
    step = 256
    for i in range(0, sums_ref.shape[0], step):
        total = None
        for t in range(hops):
            hot = hot_cols(row_ref[t : t + 1, :], i, step)
            term = mm(hot, values[t * paths : (t + 1) * paths, :])
            total = term if total is None else total + term
        sums_ref[i : i + step, :] = total.astype(BF16)


def factors_kernel(
    xs_ref, cs_ref, count_ref, wi_ref, ws_ref,
    fr_ref, fu_ref, fn_ref, fm_ref, fc_ref, cb_ref, wi_s, ws_s,
):
    t = pl.program_id(0)
    _, paths, width = xs_ref.shape
    tile = 256

    @pl.when(t == 0)
    def _():
        wi_s[...] = halved(wi_ref)
        ws_s[...] = halved(ws_ref)

    for i in range(0, paths, tile):
        at = slice(i, i + tile)
        c = cs_ref[0, at, :]
        cb = c.astype(BF16)
        cb_ref[0, at, :] = cb
        r, u, n, bn = gates(mm(xs_ref[0, at, :], wi_s[...]), mm(cb, ws_s[...]), width)
        keep = count_ref[at, :] > t
        fn = jnp.where(keep, (1.0 - u) * (1.0 - n * n), 0.0)
        fm = fn * r
        fn_ref[0, at, :] = fn
        fm_ref[0, at, :] = fm
        fr_ref[0, at, :] = fm * bn * (1.0 - r)
        fu_ref[0, at, :] = jnp.where(keep, (c - n) * u * (1.0 - u), 0.0)
        fc_ref[0, at, :] = jnp.where(keep, u, 1.0)


def turn_back(agg, w, cot):
    act = jnp.tanh(mm(agg, w))
    pre = cot.astype(F32) * (1.0 - act * act)
    high = pre.astype(BF16)
    low = (pre - high.astype(F32)).astype(BF16)
    return high, low


def link_kernel(arrived_ref, row_ref, col_ref, w_ref, cot_ref, back_ref, arrived_s, sem):
    slots = back_ref.shape[0]
    tile = 256
    arrival = pltpu.make_async_copy(arrived_ref, arrived_s, sem)
    arrival.start()
    arrival.wait()
    for i in range(0, slots, tile):
        at = slice(i, i + tile)
        same = jnp.where(col_ref[at, :] == row_ref[...], 1.0, 0.0).astype(BF16)
        agg = mm(same, arrived_s[...]).astype(BF16)
        high, low = turn_back(agg, w_ref[...], cot_ref[at, :])
        back_ref[at, :] = (mm_t(high, w_ref[...]) + mm_t(low, w_ref[...])).astype(BF16)


def link_grad_kernel(arrived_ref, row_ref, w_ref, cot_ref, out_ref):
    tile = 256
    total = None
    for i in range(0, cot_ref.shape[0], tile):
        at = slice(i, i + tile)
        agg = mm(hot_cols(row_ref[...], i, tile), arrived_ref[...]).astype(BF16)
        high, low = turn_back(agg, w_ref[...], cot_ref[at, :])
        term = t_mm(agg, high) + t_mm(agg, low)
        total = term if total is None else total + term
    out_ref[...] = total


def backward_kernel(
    table_ref, row_ref, cot_ref, wi_ref, ws_ref, agg_grad_ref,
    fr_ref, fu_ref, fn_ref, fm_ref, fc_ref, xs_ref, cb_ref,
    grad_ref, da_ref, grads_ref,
    table_s, f_s, x_s, c_s, m_s, da_s, db_s, gi_s, gs_s, sem, da_sem, table_sem,
):
    _, hops, paths, width = f_s.shape
    slots = table_ref.shape[0]
    tile = 256
    arrival = pltpu.make_async_copy(table_ref, table_s, table_sem)
    arrival.start()

    def loads(t):
        pairs = [(ref.at[t], f_s.at[k, t]) for k, ref in enumerate(
            (fr_ref, fu_ref, fn_ref, fm_ref, fc_ref))]
        pairs += [(xs_ref.at[t], x_s.at[t]), (cb_ref.at[t], c_s.at[t])]
        return [
            pltpu.make_async_copy(source, target, sem.at[k, t])
            for k, (source, target) in enumerate(pairs)
        ]

    def save(t):
        return pltpu.make_async_copy(da_s.at[t], da_ref.at[t], da_sem.at[t])

    order = list(range(hops))[::-1]
    for t in order:
        for copy in loads(t):
            copy.start()

    grad_ref[...] = cot_ref[...].astype(F32)
    arrival.wait()

    def fetch(t, i):
        at = slice(i, i + tile)
        m_s[t, at, :] = t_mm(hot_cols(row_ref[t : t + 1, at], 0, slots), table_s[...])

    def weigh(t):
        gi = t_mm(x_s[t], da_s[t])
        gs = t_mm(c_s[t], db_s[t])
        if t == hops - 1:
            gi_s[...] = gi
            gs_s[...] = gs
        else:
            gi_s[...] += gi
            gs_s[...] += gs

    for i in range(0, paths, tile):
        fetch(hops - 1, i)
    for t in order:
        for copy in loads(t):
            copy.wait()
        for i in range(0, paths, tile):
            at = slice(i, i + tile)
            if t > 0:
                fetch(t - 1, i)
            d = grad_ref[at, :] + m_s[t, at, :]
            dr = (d * f_s[0, t, at, :]).astype(BF16)
            du = (d * f_s[1, t, at, :]).astype(BF16)
            da_s[t, at, :width] = dr
            da_s[t, at, width : 2 * width] = du
            da_s[t, at, 2 * width :] = (d * f_s[2, t, at, :]).astype(BF16)
            db_s[t, at, :width] = dr
            db_s[t, at, width : 2 * width] = du
            db_s[t, at, 2 * width :] = (d * f_s[3, t, at, :]).astype(BF16)
            back = mm_t(db_s[t, at, :], ws_ref[...]).astype(BF16).astype(F32)
            grad_ref[at, :] = d * f_s[4, t, at, :] + back
        if t < hops - 1:
            weigh(t + 1)
    for t in order:
        save(t).start()
    weigh(0)
    two = 2 * width
    grads_ref[:width, :] = gi_s[:, :two].astype(BF16)
    grads_ref[width:two, :] = gs_s[:, :two].astype(BF16)
    grads_ref[two : 3 * width, :width] = gi_s[:, two:].astype(BF16)
    grads_ref[two : 3 * width, width:] = gs_s[:, two:].astype(BF16)
    grads_ref[3 * width :, :width] = agg_grad_ref[...].astype(BF16)
    grads_ref[3 * width :, width:] = jnp.zeros_like(agg_grad_ref).astype(BF16)
    for t in order:
        save(t).wait()


def input_kernel(da_ref, row_ref, wi_ref, sums_ref, dx_s):
    hops, paths, _ = da_ref.shape
    for t in range(hops):
        dx_s[t * paths : (t + 1) * paths, :] = mm_t(da_ref[t], wi_ref[...]).astype(BF16)
    add_up(row_ref, dx_s, sums_ref)


def share_kernel(devices, parts_ref, sums_ref, out_ref):
    slots, wide = parts_ref.shape
    width = sums_ref.shape[1]
    lines = slots // devices
    total = jnp.sum(parts_ref[...].reshape(devices // 2, 2 * lines, wide).astype(F32), axis=0)
    total = total[:lines] + total[lines:]
    pair = jnp.concatenate([total, total], axis=0).astype(BF16)
    out_ref[:, :width] = sums_ref[...]
    out_ref[:, width:] = jnp.broadcast_to(pair[None], (devices // 2, 2 * lines, wide)).reshape(slots, wide)


def final_kernel(
    path_scale, link_scale, got_ref, row_ref, cot_ref,
    link_ref, gi_ref, gs_ref, ga_ref, got_s, out_s, sem, out_sem,
):
    width = ga_ref.shape[0]
    links = cot_ref.shape[0]
    two = 2 * width
    tile = 512
    arrival = pltpu.make_async_copy(got_ref, got_s, sem)
    arrival.start()
    arrival.wait()

    def save(k):
        at = pl.ds(k * tile, tile)
        return pltpu.make_async_copy(out_s.at[at, :], link_ref.at[at, :], out_sem.at[k])

    for k in range(links // tile):
        at = slice(k * tile, (k + 1) * tile)
        total = mm(hot_cols(row_ref[...], k * tile, tile), got_s[:, :width])
        out_s[at, :] = cot_ref[at, :].astype(F32) + total
        save(k).start()
    gi_ref[:, :two] = got_s[:width, width:].astype(F32) * path_scale
    gs_ref[:, :two] = got_s[width:two, width:].astype(F32) * path_scale
    gi_ref[:, two:] = got_s[two : 3 * width, width:two].astype(F32) * path_scale
    gs_ref[:, two:] = got_s[two : 3 * width, two:].astype(F32) * path_scale
    ga_ref[...] = got_s[3 * width :, width:two].astype(F32) * link_scale
    for k in range(links // tile):
        save(k).wait()


def exchange(rows, devices):
    lines, width = rows.shape
    chunks = rows.reshape(devices, lines // devices, width)
    got = lax.all_to_all(chunks, AXES, split_axis=0, concat_axis=0, tiled=True)
    return got.reshape(lines, width)


def per_device(
    path_state, link_state, hop_slot, hop_count, send_rows,
    w_input, w_state, w_agg, path_cot, link_cot,
):
    devices = lax.axis_size("outer") * lax.axis_size("sw")
    paths, width = path_state.shape
    hops = hop_slot.shape[1]
    links = link_state.shape[0]
    slots = devices * send_rows.shape[1]
    gate_cols = w_input.shape[1]
    shape = jax.ShapeDtypeStruct

    slot_rows = shape((slots, width), BF16)
    rows, send_row = call(
        pick_kernel, (slot_rows, shape((1, slots), jnp.int32)), [],
        (2 * slots * links * width, 2 * links * width, 16), send_rows.T, link_state,
    )
    table = exchange(rows, devices)

    valid = jnp.arange(hops, dtype=jnp.int32)[:, None] < hop_count[None, :]
    slot_row = jnp.where(valid, hop_slot.T, -1)
    count = hop_count[:, None]
    send_col = send_rows.reshape(slots, 1)
    cot_rows = call(
        pick_again_kernel, slot_rows, [],
        (2 * slots * links * width, 2 * links * width, 16), send_row, link_cot,
    )
    table, cot_rows, send_col, count, slot_row = lax.optimization_barrier(
        (table, cot_rows, send_col, count, slot_row)
    )
    sums, xs, cs = call(
        forward_kernel,
        (slot_rows, shape((hops, paths, width), BF16), shape((hops, paths, width), F32)),
        [
            pltpu.VMEM((slots, width), BF16),
            pltpu.VMEM((width, gate_cols), BF16),
            pltpu.VMEM((width, gate_cols), BF16),
            pltpu.VMEM((hops, paths, gate_cols), F32),
            pltpu.VMEM((hops, paths, width), BF16),
            pltpu.VMEM((hops, paths, width), F32),
            pltpu.VMEM((hops * paths, width), BF16),
            pltpu.SemaphoreType.DMA((2, hops)),
            pltpu.SemaphoreType.DMA,
        ],
        (4 * hops * paths * slots * width, 8 * hops * paths * width, 58),
        table, count, slot_row, path_state, w_input, w_state,
        in_specs=[ANY] + [VMEM] * 5,
        out_specs=(VMEM, ANY, ANY),
    )
    arrived = exchange(sums, devices)

    whole = lambda *dims: pl.BlockSpec(dims, lambda i: (0,) * len(dims))
    factor = shape((hops, paths, width), F32)
    hop_block = pl.BlockSpec((1, paths, width), lambda i: (i, 0, 0))
    factors = pl.pallas_call(
        factors_kernel,
        grid=(hops,),
        out_shape=(factor,) * 5 + (shape((hops, paths, width), BF16),),
        in_specs=[
            hop_block, hop_block, whole(paths, 1),
            whole(width, gate_cols), whole(width, gate_cols),
        ],
        out_specs=(hop_block,) * 6,
        scratch_shapes=[pltpu.VMEM((width, gate_cols), BF16)] * 2,
        compiler_params=pltpu.CompilerParams(vmem_limit_bytes=58 * MIB),
        cost_estimate=pl.CostEstimate(
            flops=4 * hops * paths * width * gate_cols,
            bytes_accessed=32 * hops * paths * width, transcendentals=0,
        ),
    )(xs, cs, count, w_input, w_state)
    arrived, factors = lax.optimization_barrier((arrived, factors))

    back = call(
        link_kernel, slot_rows,
        [pltpu.VMEM((slots, width), BF16), pltpu.SemaphoreType.DMA],
        (2 * slots * slots * width, 8 * slots * width, 16),
        arrived, send_row, send_col, w_agg, cot_rows,
        in_specs=[ANY] + [VMEM] * 4,
    )
    back_table = exchange(back, devices)
    agg_grad = call(
        link_grad_kernel, shape((width, width), F32), [],
        (4 * links * width * width, 6 * links * width, 16), arrived, send_row, w_agg, link_cot,
    )
    back_table, agg_grad = lax.optimization_barrier((back_table, agg_grad))

    grad_path, da, grads = call(
        backward_kernel,
        (
            shape((paths, width), F32),
            shape((hops, paths, gate_cols), BF16),
            shape((4 * width, 2 * width), BF16),
        ),
        [
            pltpu.VMEM((slots, width), BF16),
            pltpu.VMEM((5, hops, paths, width), F32),
            pltpu.VMEM((hops, paths, width), BF16),
            pltpu.VMEM((hops, paths, width), BF16),
            pltpu.VMEM((hops, paths, width), F32),
            pltpu.VMEM((hops, paths, gate_cols), BF16),
            pltpu.VMEM((hops, paths, gate_cols), BF16),
            pltpu.VMEM((width, gate_cols), F32),
            pltpu.VMEM((width, gate_cols), F32),
            pltpu.SemaphoreType.DMA((7, hops)),
            pltpu.SemaphoreType.DMA((hops,)),
            pltpu.SemaphoreType.DMA,
        ],
        (10 * hops * paths * width * gate_cols, 32 * hops * paths * width, 52),
        back_table, slot_row, path_cot, w_input, w_state, agg_grad,
        *factors[:5], xs, factors[5],
        in_specs=[ANY] + [VMEM] * 5 + [ANY] * 7,
        out_specs=(VMEM, ANY, VMEM),
    )
    parts = exchange(grads, devices)
    input_sums = call(
        input_kernel, slot_rows, [pltpu.VMEM((hops * paths, width), BF16)],
        (2 * hops * paths * (gate_cols + slots) * width, 2 * hops * paths * gate_cols, 24),
        da, slot_row, w_input,
    )
    parts, input_sums = lax.optimization_barrier((parts, input_sums))
    last = call(
        functools.partial(share_kernel, devices), shape((slots, 3 * width), BF16), [],
        (slots * width, 10 * slots * width, 16), parts, input_sums,
    )
    got = exchange(last, devices)
    wide = shape((width, gate_cols), F32)
    grad_link, input_grad, state_grad, agg_total = call(
        functools.partial(
            final_kernel, 1.0 / math.sqrt(paths * devices), 1.0 / math.sqrt(links * devices)
        ),
        (shape((links, width), F32), wide, wide, shape((width, width), F32)),
        [
            pltpu.VMEM((slots, 3 * width), BF16),
            pltpu.VMEM((links, width), F32),
            pltpu.SemaphoreType.DMA,
            pltpu.SemaphoreType.DMA((links // 512,)),
        ],
        (2 * slots * links * width, 8 * links * width, 16),
        got, send_row, link_cot,
        in_specs=[ANY, VMEM, VMEM],
        out_specs=(ANY, VMEM, VMEM, VMEM),
    )
    return grad_path, grad_link, input_grad, state_grad, agg_total


def solution(mesh):
    split = P(AXES, None)
    return jax.shard_map(
        per_device,
        mesh=mesh,
        in_specs=(split, split, split, P(AXES), split, P(), P(), P(), split, split),
        out_specs=(split, split, P(), P(), P()),
        check_vma=False,
    )
```

```python
import functools
import math

import jax
import jax.numpy as jnp
from jax import lax
from jax.experimental import pallas as pl
from jax.experimental.pallas import tpu as pltpu
from jax.sharding import PartitionSpec as P

F32 = jnp.float32
BF16 = jnp.bfloat16
AXES = ("outer", "sw")
MIB = 1024 * 1024
VMEM = pl.BlockSpec(memory_space=pltpu.VMEM)
ANY = pl.BlockSpec(memory_space=pl.ANY)


def mm(a, b):
    return lax.dot_general(a, b, (((1,), (0,)), ((), ())), preferred_element_type=F32)


def mm_t(a, b):
    return lax.dot_general(a, b, (((1,), (1,)), ((), ())), preferred_element_type=F32)


def t_mm(a, b):
    return lax.dot_general(a, b, (((0,), (0,)), ((), ())), preferred_element_type=F32)


def hot_cols(row, start, height):
    lines = lax.broadcasted_iota(jnp.int32, (height, row.shape[1]), 0) + start
    return jnp.where(row == lines, 1.0, 0.0).astype(BF16)


def call(kernel, outs, scratch, cost, *args, in_specs=None, out_specs=None):
    flops, moved, room = cost
    return pl.pallas_call(
        kernel,
        out_shape=outs,
        in_specs=in_specs or [VMEM] * len(args),
        out_specs=out_specs or jax.tree.map(lambda _: VMEM, outs),
        scratch_shapes=scratch,
        compiler_params=pltpu.CompilerParams(vmem_limit_bytes=room * MIB),
        cost_estimate=pl.CostEstimate(flops=flops, bytes_accessed=moved, transcendentals=0),
    )(*args)


def pick_kernel(turned_ref, link_ref, out_ref, row_ref):
    capacity, devices = turned_ref.shape
    slots = capacity * devices
    links = link_ref.shape[0]
    listed = turned_ref[...]
    high = (listed >> 8).astype(F32).astype(BF16)
    low = (listed & 255).astype(F32).astype(BF16)
    owner = lax.broadcasted_iota(jnp.int32, (devices, slots), 0)
    place = lax.broadcasted_iota(jnp.int32, (devices, slots), 1)
    spread = jnp.where(place // capacity == owner, 1.0, 0.0).astype(BF16)
    wide = mm(high, spread) * 256.0 + mm(low, spread)
    line = lax.broadcasted_iota(jnp.int32, (capacity, slots), 0)
    at = lax.broadcasted_iota(jnp.int32, (capacity, slots), 1)
    row = jnp.sum(jnp.where(at % capacity == line, wide, 0.0), axis=0, keepdims=True)
    row_ref[...] = row.astype(jnp.int32)
    step = 512
    total = None
    for i in range(0, links, step):
        term = t_mm(hot_cols(row_ref[...], i, step), link_ref[i : i + step, :])
        total = term if total is None else total + term
    out_ref[...] = total.astype(BF16)


def pick_again_kernel(row_ref, link_ref, out_ref):
    step = 512
    total = None
    for i in range(0, link_ref.shape[0], step):
        term = t_mm(hot_cols(row_ref[...], i, step), link_ref[i : i + step, :])
        total = term if total is None else total + term
    out_ref[...] = total.astype(BF16)


def halved(w_ref):
    width = w_ref.shape[0]
    lanes = lax.broadcasted_iota(jnp.int32, w_ref.shape, 1)
    w = w_ref[...].astype(F32)
    return jnp.where(lanes < 2 * width, 0.5 * w, w).astype(BF16)


def gates(a, b, width):
    r = 0.5 * jnp.tanh(a[:, :width] + b[:, :width]) + 0.5
    u = 0.5 * jnp.tanh(a[:, width : 2 * width] + b[:, width : 2 * width]) + 0.5
    bn = b[:, 2 * width :]
    n = jnp.tanh(a[:, 2 * width :] + r * bn)
    return r, u, n, bn


def forward_kernel(
    table_ref, count_ref, row_ref, start_ref, wi_ref, ws_ref,
    sums_ref, xs_ref, cs_ref, table_s, wi_s, ws_s, a_s, x_s, c_s, msg_s, sem, table_sem,
):
    hops, paths, width = x_s.shape
    slots = table_ref.shape[0]
    tile = 256
    arrival = pltpu.make_async_copy(table_ref, table_s, table_sem)
    arrival.start()
    wi_s[...] = halved(wi_ref)
    ws_s[...] = halved(ws_ref)
    c_s[0] = start_ref[...].astype(F32)
    arrival.wait()

    def saves(t):
        return (
            pltpu.make_async_copy(x_s.at[t], xs_ref.at[t], sem.at[0, t]),
            pltpu.make_async_copy(c_s.at[t], cs_ref.at[t], sem.at[1, t]),
        )

    for t in range(hops):
        hot = hot_cols(row_ref[t : t + 1, :], 0, slots)
        x_s[t] = t_mm(hot, table_s[...]).astype(BF16)

    a_s[0] = mm(x_s[0], wi_s[...])
    for t in range(hops):
        if t + 1 < hops:
            a_s[t + 1] = mm(x_s[t + 1], wi_s[...])
        for i in range(0, paths, tile):
            at = slice(i, i + tile)
            c = c_s[t, at, :]
            b = mm(c.astype(BF16), ws_s[...])
            r, u, n, _ = gates(a_s[t, at, :], b, width)
            c = jnp.where(count_ref[at, :] > t, n + u * (c - n), c)
            if t + 1 < hops:
                c_s[t + 1, at, :] = c
            msg_s[t * paths + i : t * paths + i + tile, :] = c.astype(BF16)
    for t in range(hops):
        for copy in saves(t):
            copy.start()

    add_up(row_ref, msg_s, sums_ref)
    for t in range(hops):
        for copy in saves(t):
            copy.wait()


def add_up(row_ref, values, sums_ref):
    hops, paths = row_ref.shape
    step = 256
    for i in range(0, sums_ref.shape[0], step):
        total = None
        for t in range(hops):
            hot = hot_cols(row_ref[t : t + 1, :], i, step)
            term = mm(hot, values[t * paths : (t + 1) * paths, :])
            total = term if total is None else total + term
        sums_ref[i : i + step, :] = total.astype(BF16)


def factors_kernel(
    xs_ref, cs_ref, count_ref, wi_ref, ws_ref,
    fr_ref, fu_ref, fn_ref, fm_ref, fc_ref, cb_ref, wi_s, ws_s,
):
    t = pl.program_id(0)
    _, paths, width = xs_ref.shape
    tile = 256

    @pl.when(t == 0)
    def _():
        wi_s[...] = halved(wi_ref)
        ws_s[...] = halved(ws_ref)

    for i in range(0, paths, tile):
        at = slice(i, i + tile)
        c = cs_ref[0, at, :]
        cb = c.astype(BF16)
        cb_ref[0, at, :] = cb
        r, u, n, bn = gates(mm(xs_ref[0, at, :], wi_s[...]), mm(cb, ws_s[...]), width)
        keep = count_ref[at, :] > t
        fn = jnp.where(keep, (1.0 - u) * (1.0 - n * n), 0.0)
        fm = fn * r
        fn_ref[0, at, :] = fn.astype(BF16)
        fm_ref[0, at, :] = fm.astype(BF16)
        fr_ref[0, at, :] = (fm * bn * (1.0 - r)).astype(BF16)
        fu_ref[0, at, :] = jnp.where(keep, (c - n) * u * (1.0 - u), 0.0).astype(BF16)
        fc_ref[0, at, :] = jnp.where(keep, u, 1.0)


def turn_back(agg, w, cot):
    act = jnp.tanh(mm(agg, w))
    pre = cot.astype(F32) * (1.0 - act * act)
    high = pre.astype(BF16)
    low = (pre - high.astype(F32)).astype(BF16)
    return high, low


def link_kernel(arrived_ref, row_ref, col_ref, w_ref, cot_ref, back_ref, arrived_s, sem):
    slots = back_ref.shape[0]
    tile = 256
    arrival = pltpu.make_async_copy(arrived_ref, arrived_s, sem)
    arrival.start()
    arrival.wait()
    for i in range(0, slots, tile):
        at = slice(i, i + tile)
        same = jnp.where(col_ref[at, :] == row_ref[...], 1.0, 0.0).astype(BF16)
        agg = mm(same, arrived_s[...]).astype(BF16)
        high, low = turn_back(agg, w_ref[...], cot_ref[at, :])
        back_ref[at, :] = (mm_t(high, w_ref[...]) + mm_t(low, w_ref[...])).astype(BF16)


def link_grad_kernel(arrived_ref, row_ref, w_ref, cot_ref, out_ref):
    tile = 256
    total = None
    for i in range(0, cot_ref.shape[0], tile):
        at = slice(i, i + tile)
        agg = mm(hot_cols(row_ref[...], i, tile), arrived_ref[...]).astype(BF16)
        high, low = turn_back(agg, w_ref[...], cot_ref[at, :])
        term = t_mm(agg, high) + t_mm(agg, low)
        total = term if total is None else total + term
    out_ref[...] = total


def backward_kernel(
    table_ref, row_ref, cot_ref, wi_ref, ws_ref, agg_grad_ref,
    fr_ref, fu_ref, fn_ref, fm_ref, fc_ref, xs_ref, cb_ref,
    grad_ref, da_ref, grads_ref,
    table_s, f_s, fc_s, x_s, c_s, m_s, da_s, db_s, gi_s, gs_s, sem, da_sem, table_sem,
):
    _, hops, paths, width = f_s.shape
    slots = table_ref.shape[0]
    tile = 256
    arrival = pltpu.make_async_copy(table_ref, table_s, table_sem)
    arrival.start()

    def loads(t):
        pairs = [(ref.at[t], f_s.at[k, t]) for k, ref in enumerate(
            (fr_ref, fu_ref, fn_ref, fm_ref))]
        pairs += [
            (fc_ref.at[t], fc_s.at[t]), (xs_ref.at[t], x_s.at[t]), (cb_ref.at[t], c_s.at[t]),
        ]
        return [
            pltpu.make_async_copy(source, target, sem.at[k, t])
            for k, (source, target) in enumerate(pairs)
        ]

    def save(t):
        return pltpu.make_async_copy(da_s.at[t], da_ref.at[t], da_sem.at[t])

    order = list(range(hops))[::-1]
    for t in order:
        for copy in loads(t):
            copy.start()

    grad_ref[...] = cot_ref[...].astype(F32)
    arrival.wait()

    for t in order:
        m_s[t] = t_mm(hot_cols(row_ref[t : t + 1, :], 0, slots), table_s[...])
    for t in order:
        for copy in loads(t):
            copy.wait()
        for i in range(0, paths, tile):
            at = slice(i, i + tile)
            d = grad_ref[at, :] + m_s[t, at, :]
            dr = (d * f_s[0, t, at, :]).astype(BF16)
            du = (d * f_s[1, t, at, :]).astype(BF16)
            da_s[t, at, :width] = dr
            da_s[t, at, width : 2 * width] = du
            da_s[t, at, 2 * width :] = (d * f_s[2, t, at, :]).astype(BF16)
            db_s[t, at, :width] = dr
            db_s[t, at, width : 2 * width] = du
            db_s[t, at, 2 * width :] = (d * f_s[3, t, at, :]).astype(BF16)
            back = mm_t(db_s[t, at, :], ws_ref[...]).astype(BF16).astype(F32)
            grad_ref[at, :] = d * fc_s[t, at, :] + back
        save(t).start()
    gi_s[...] = t_mm(flat(x_s), flat(da_s))
    gs_s[...] = t_mm(flat(c_s), flat(db_s))
    two = 2 * width
    grads_ref[:width, :] = gi_s[:, :two].astype(BF16)
    grads_ref[width:two, :] = gs_s[:, :two].astype(BF16)
    grads_ref[two : 3 * width, :width] = gi_s[:, two:].astype(BF16)
    grads_ref[two : 3 * width, width:] = gs_s[:, two:].astype(BF16)
    grads_ref[3 * width :, :width] = agg_grad_ref[...].astype(BF16)
    grads_ref[3 * width :, width:] = jnp.zeros_like(agg_grad_ref).astype(BF16)
    for t in order:
        save(t).wait()


def flat(ref):
    hops, paths, width = ref.shape
    return ref[...].reshape(hops * paths, width)


def input_kernel(da_ref, row_ref, wi_ref, sums_ref, dx_s):
    hops, paths, _ = da_ref.shape
    for t in range(hops):
        dx_s[t * paths : (t + 1) * paths, :] = mm_t(da_ref[t], wi_ref[...]).astype(BF16)
    add_up(row_ref, dx_s, sums_ref)


def share_kernel(devices, parts_ref, sums_ref, out_ref):
    slots, wide = parts_ref.shape
    width = sums_ref.shape[1]
    lines = slots // devices
    total = jnp.sum(parts_ref[...].reshape(devices // 2, 2 * lines, wide).astype(F32), axis=0)
    total = total[:lines] + total[lines:]
    pair = jnp.concatenate([total, total], axis=0).astype(BF16)
    out_ref[:, :width] = sums_ref[...]
    out_ref[:, width:] = jnp.broadcast_to(pair[None], (devices // 2, 2 * lines, wide)).reshape(slots, wide)


def final_kernel(
    path_scale, link_scale, got_ref, row_ref, cot_ref,
    link_ref, gi_ref, gs_ref, ga_ref, got_s, out_s, sem, out_sem,
):
    width = ga_ref.shape[0]
    links = cot_ref.shape[0]
    two = 2 * width
    tile = 512
    arrival = pltpu.make_async_copy(got_ref, got_s, sem)
    arrival.start()
    arrival.wait()

    def save(k):
        at = pl.ds(k * tile, tile)
        return pltpu.make_async_copy(out_s.at[at, :], link_ref.at[at, :], out_sem.at[k])

    for k in range(links // tile):
        at = slice(k * tile, (k + 1) * tile)
        total = mm(hot_cols(row_ref[...], k * tile, tile), got_s[:, :width])
        out_s[at, :] = cot_ref[at, :].astype(F32) + total
        save(k).start()
    gi_ref[:, :two] = got_s[:width, width:].astype(F32) * path_scale
    gs_ref[:, :two] = got_s[width:two, width:].astype(F32) * path_scale
    gi_ref[:, two:] = got_s[two : 3 * width, width:two].astype(F32) * path_scale
    gs_ref[:, two:] = got_s[two : 3 * width, two:].astype(F32) * path_scale
    ga_ref[...] = got_s[3 * width :, width:two].astype(F32) * link_scale
    for k in range(links // tile):
        save(k).wait()


def exchange(rows, devices):
    lines, width = rows.shape
    chunks = rows.reshape(devices, lines // devices, width)
    got = lax.all_to_all(chunks, AXES, split_axis=0, concat_axis=0, tiled=True)
    return got.reshape(lines, width)


def per_device(
    path_state, link_state, hop_slot, hop_count, send_rows,
    w_input, w_state, w_agg, path_cot, link_cot,
):
    devices = lax.axis_size("outer") * lax.axis_size("sw")
    paths, width = path_state.shape
    hops = hop_slot.shape[1]
    links = link_state.shape[0]
    slots = devices * send_rows.shape[1]
    gate_cols = w_input.shape[1]
    shape = jax.ShapeDtypeStruct

    slot_rows = shape((slots, width), BF16)
    rows, send_row = call(
        pick_kernel, (slot_rows, shape((1, slots), jnp.int32)), [],
        (2 * slots * links * width, 2 * links * width, 16), send_rows.T, link_state,
    )
    table = exchange(rows, devices)

    valid = jnp.arange(hops, dtype=jnp.int32)[:, None] < hop_count[None, :]
    slot_row = jnp.where(valid, hop_slot.T, -1)
    count = hop_count[:, None]
    send_col = send_rows.reshape(slots, 1)
    cot_rows = call(
        pick_again_kernel, slot_rows, [],
        (2 * slots * links * width, 2 * links * width, 16), send_row, link_cot,
    )
    table, cot_rows, send_col, count, slot_row = lax.optimization_barrier(
        (table, cot_rows, send_col, count, slot_row)
    )
    sums, xs, cs = call(
        forward_kernel,
        (slot_rows, shape((hops, paths, width), BF16), shape((hops, paths, width), F32)),
        [
            pltpu.VMEM((slots, width), BF16),
            pltpu.VMEM((width, gate_cols), BF16),
            pltpu.VMEM((width, gate_cols), BF16),
            pltpu.VMEM((hops, paths, gate_cols), F32),
            pltpu.VMEM((hops, paths, width), BF16),
            pltpu.VMEM((hops, paths, width), F32),
            pltpu.VMEM((hops * paths, width), BF16),
            pltpu.SemaphoreType.DMA((2, hops)),
            pltpu.SemaphoreType.DMA,
        ],
        (4 * hops * paths * slots * width, 8 * hops * paths * width, 58),
        table, count, slot_row, path_state, w_input, w_state,
        in_specs=[ANY] + [VMEM] * 5,
        out_specs=(VMEM, ANY, ANY),
    )
    arrived = exchange(sums, devices)

    whole = lambda *dims: pl.BlockSpec(dims, lambda i: (0,) * len(dims))
    factor = shape((hops, paths, width), F32)
    short = shape((hops, paths, width), BF16)
    hop_block = pl.BlockSpec((1, paths, width), lambda i: (i, 0, 0))
    factors = pl.pallas_call(
        factors_kernel,
        grid=(hops,),
        out_shape=(short,) * 4 + (factor, short),
        in_specs=[
            hop_block, hop_block, whole(paths, 1),
            whole(width, gate_cols), whole(width, gate_cols),
        ],
        out_specs=(hop_block,) * 6,
        scratch_shapes=[pltpu.VMEM((width, gate_cols), BF16)] * 2,
        compiler_params=pltpu.CompilerParams(vmem_limit_bytes=58 * MIB),
        cost_estimate=pl.CostEstimate(
            flops=4 * hops * paths * width * gate_cols,
            bytes_accessed=32 * hops * paths * width, transcendentals=0,
        ),
    )(xs, cs, count, w_input, w_state)
    arrived, factors = lax.optimization_barrier((arrived, factors))

    back = call(
        link_kernel, slot_rows,
        [pltpu.VMEM((slots, width), BF16), pltpu.SemaphoreType.DMA],
        (2 * slots * slots * width, 8 * slots * width, 16),
        arrived, send_row, send_col, w_agg, cot_rows,
        in_specs=[ANY] + [VMEM] * 4,
    )
    back_table = exchange(back, devices)
    agg_grad = call(
        link_grad_kernel, shape((width, width), F32), [],
        (4 * links * width * width, 6 * links * width, 16), arrived, send_row, w_agg, link_cot,
    )
    back_table, agg_grad = lax.optimization_barrier((back_table, agg_grad))

    grad_path, da, grads = call(
        backward_kernel,
        (
            shape((paths, width), F32),
            shape((hops, paths, gate_cols), BF16),
            shape((4 * width, 2 * width), BF16),
        ),
        [
            pltpu.VMEM((slots, width), BF16),
            pltpu.VMEM((4, hops, paths, width), BF16),
            pltpu.VMEM((hops, paths, width), F32),
            pltpu.VMEM((hops, paths, width), BF16),
            pltpu.VMEM((hops, paths, width), BF16),
            pltpu.VMEM((hops, paths, width), F32),
            pltpu.VMEM((hops, paths, gate_cols), BF16),
            pltpu.VMEM((hops, paths, gate_cols), BF16),
            pltpu.VMEM((width, gate_cols), F32),
            pltpu.VMEM((width, gate_cols), F32),
            pltpu.SemaphoreType.DMA((7, hops)),
            pltpu.SemaphoreType.DMA((hops,)),
            pltpu.SemaphoreType.DMA,
        ],
        (10 * hops * paths * width * gate_cols, 32 * hops * paths * width, 52),
        back_table, slot_row, path_cot, w_input, w_state, agg_grad,
        *factors[:5], xs, factors[5],
        in_specs=[ANY] + [VMEM] * 5 + [ANY] * 7,
        out_specs=(VMEM, ANY, VMEM),
    )
    parts = exchange(grads, devices)
    input_sums = call(
        input_kernel, slot_rows, [pltpu.VMEM((hops * paths, width), BF16)],
        (2 * hops * paths * (gate_cols + slots) * width, 2 * hops * paths * gate_cols, 24),
        da, slot_row, w_input,
    )
    parts, input_sums = lax.optimization_barrier((parts, input_sums))
    last = call(
        functools.partial(share_kernel, devices), shape((slots, 3 * width), BF16), [],
        (slots * width, 10 * slots * width, 16), parts, input_sums,
    )
    got = exchange(last, devices)
    wide = shape((width, gate_cols), F32)
    grad_link, input_grad, state_grad, agg_total = call(
        functools.partial(
            final_kernel, 1.0 / math.sqrt(paths * devices), 1.0 / math.sqrt(links * devices)
        ),
        (shape((links, width), F32), wide, wide, shape((width, width), F32)),
        [
            pltpu.VMEM((slots, 3 * width), BF16),
            pltpu.VMEM((links, width), F32),
            pltpu.SemaphoreType.DMA,
            pltpu.SemaphoreType.DMA((links // 512,)),
        ],
        (2 * slots * links * width, 8 * links * width, 16),
        got, send_row, link_cot,
        in_specs=[ANY, VMEM, VMEM],
        out_specs=(ANY, VMEM, VMEM, VMEM),
    )
    return grad_path, grad_link, input_grad, state_grad, agg_total


def solution(mesh):
    split = P(AXES, None)
    return jax.shard_map(
        per_device,
        mesh=mesh,
        in_specs=(split, split, split, P(AXES), split, P(), P(), P(), split, split),
        out_specs=(split, split, P(), P(), P()),
        check_vma=False,
    )
```

```python
import functools
import math

import jax
import jax.numpy as jnp
from jax import lax
from jax.experimental import pallas as pl
from jax.experimental.pallas import tpu as pltpu
from jax.sharding import Mesh
from jax.sharding import PartitionSpec as P

F32 = jnp.float32
BF16 = jnp.bfloat16
AXES = ("group", "core", "sw")
CHIPS = ("group", "sw")
MIB = 1024 * 1024
VMEM = pl.BlockSpec(memory_space=pltpu.VMEM)
ANY = pl.BlockSpec(memory_space=pl.ANY)
SMEM = pl.BlockSpec(memory_space=pltpu.SMEM)


def mm(a, b):
    return lax.dot_general(a, b, (((1,), (0,)), ((), ())), preferred_element_type=F32)


def mm_t(a, b):
    return lax.dot_general(a, b, (((1,), (1,)), ((), ())), preferred_element_type=F32)


def t_mm(a, b):
    return lax.dot_general(a, b, (((0,), (0,)), ((), ())), preferred_element_type=F32)


def hot_cols(row, start, height):
    lines = lax.broadcasted_iota(jnp.int32, (height, row.shape[1]), 0) + start
    return jnp.where(row == lines, 1.0, 0.0).astype(BF16)


def call(kernel, outs, scratch, cost, *args, in_specs=None, out_specs=None):
    flops, moved, room = cost
    return pl.pallas_call(
        kernel,
        out_shape=outs,
        in_specs=in_specs or [VMEM] * len(args),
        out_specs=out_specs or jax.tree.map(lambda _: VMEM, outs),
        scratch_shapes=scratch,
        compiler_params=pltpu.CompilerParams(vmem_limit_bytes=room * MIB),
        cost_estimate=pl.CostEstimate(flops=flops, bytes_accessed=moved, transcendentals=0),
    )(*args)


def pick_kernel(turned_ref, link_ref, out_ref, row_ref):
    capacity, devices = turned_ref.shape
    slots = capacity * devices
    links = link_ref.shape[0]
    listed = turned_ref[...]
    high = (listed >> 8).astype(F32).astype(BF16)
    low = (listed & 255).astype(F32).astype(BF16)
    owner = lax.broadcasted_iota(jnp.int32, (devices, slots), 0)
    place = lax.broadcasted_iota(jnp.int32, (devices, slots), 1)
    spread = jnp.where(place // capacity == owner, 1.0, 0.0).astype(BF16)
    wide = mm(high, spread) * 256.0 + mm(low, spread)
    line = lax.broadcasted_iota(jnp.int32, (capacity, slots), 0)
    at = lax.broadcasted_iota(jnp.int32, (capacity, slots), 1)
    row = jnp.sum(jnp.where(at % capacity == line, wide, 0.0), axis=0, keepdims=True)
    row_ref[...] = row.astype(jnp.int32)
    step = 512
    total = None
    for i in range(0, links, step):
        term = t_mm(hot_cols(row_ref[...], i, step), link_ref[i : i + step, :])
        total = term if total is None else total + term
    out_ref[...] = total.astype(BF16)


def pick_again_kernel(row_ref, link_ref, out_ref):
    step = 512
    total = None
    for i in range(0, link_ref.shape[0], step):
        term = t_mm(hot_cols(row_ref[...], i, step), link_ref[i : i + step, :])
        total = term if total is None else total + term
    out_ref[...] = total.astype(BF16)


def halved(w_ref):
    width = w_ref.shape[0]
    lanes = lax.broadcasted_iota(jnp.int32, w_ref.shape, 1)
    w = w_ref[...].astype(F32)
    return jnp.where(lanes < 2 * width, 0.5 * w, w).astype(BF16)


def gates(a, b, width):
    r = 0.5 * jnp.tanh(a[:, :width] + b[:, :width]) + 0.5
    u = 0.5 * jnp.tanh(a[:, width : 2 * width] + b[:, width : 2 * width]) + 0.5
    bn = b[:, 2 * width :]
    n = jnp.tanh(a[:, 2 * width :] + r * bn)
    return r, u, n, bn


def forward_kernel(
    table_ref, count_ref, row_ref, start_ref, wi_ref, ws_ref,
    sums_ref, xs_ref, cs_ref, table_s, wi_s, ws_s, a_s, x_s, c_s, msg_s, sem, table_sem,
):
    hops, paths, width = x_s.shape
    slots = table_ref.shape[0]
    tile = 256
    arrival = pltpu.make_async_copy(table_ref, table_s, table_sem)
    arrival.start()
    wi_s[...] = halved(wi_ref)
    ws_s[...] = halved(ws_ref)
    c_s[0] = start_ref[...].astype(F32)
    arrival.wait()

    def saves(t):
        return (
            pltpu.make_async_copy(x_s.at[t], xs_ref.at[t], sem.at[0, t]),
            pltpu.make_async_copy(c_s.at[t], cs_ref.at[t], sem.at[1, t]),
        )

    for t in range(hops):
        hot = hot_cols(row_ref[t : t + 1, :], 0, slots)
        x_s[t] = t_mm(hot, table_s[...]).astype(BF16)

    a_s[0] = mm(x_s[0], wi_s[...])
    for t in range(hops):
        if t + 1 < hops:
            a_s[t + 1] = mm(x_s[t + 1], wi_s[...])
        for i in range(0, paths, tile):
            at = slice(i, i + tile)
            c = c_s[t, at, :]
            b = mm(c.astype(BF16), ws_s[...])
            r, u, n, _ = gates(a_s[t, at, :], b, width)
            c = jnp.where(count_ref[at, :] > t, n + u * (c - n), c)
            if t + 1 < hops:
                c_s[t + 1, at, :] = c
            msg_s[t * paths + i : t * paths + i + tile, :] = c.astype(BF16)
    for t in range(hops):
        for copy in saves(t):
            copy.start()

    add_up(row_ref, msg_s, sums_ref)
    for t in range(hops):
        for copy in saves(t):
            copy.wait()


def add_up(row_ref, values, sums_ref):
    hops, paths = row_ref.shape
    step = 256
    for i in range(0, sums_ref.shape[0], step):
        total = None
        for t in range(hops):
            hot = hot_cols(row_ref[t : t + 1, :], i, step)
            term = mm(hot, values[t * paths : (t + 1) * paths, :])
            total = term if total is None else total + term
        sums_ref[i : i + step, :] = total.astype(BF16)


def factors_kernel(
    xs_ref, cs_ref, count_ref, wi_ref, ws_ref,
    fr_ref, fu_ref, fn_ref, fm_ref, fc_ref, cb_ref, wi_s, ws_s,
):
    t = pl.program_id(0)
    _, paths, width = xs_ref.shape
    tile = 256

    @pl.when(t == 0)
    def _():
        wi_s[...] = halved(wi_ref)
        ws_s[...] = halved(ws_ref)

    for i in range(0, paths, tile):
        at = slice(i, i + tile)
        c = cs_ref[0, at, :]
        cb = c.astype(BF16)
        cb_ref[0, at, :] = cb
        r, u, n, bn = gates(mm(xs_ref[0, at, :], wi_s[...]), mm(cb, ws_s[...]), width)
        keep = count_ref[at, :] > t
        fn = jnp.where(keep, (1.0 - u) * (1.0 - n * n), 0.0)
        fm = fn * r
        fn_ref[0, at, :] = fn.astype(BF16)
        fm_ref[0, at, :] = fm.astype(BF16)
        fr_ref[0, at, :] = (fm * bn * (1.0 - r)).astype(BF16)
        fu_ref[0, at, :] = jnp.where(keep, (c - n) * u * (1.0 - u), 0.0).astype(BF16)
        fc_ref[0, at, :] = jnp.where(keep, u, 1.0)


def turn_back(agg, w, cot):
    act = jnp.tanh(mm(agg, w))
    pre = cot.astype(F32) * (1.0 - act * act)
    high = pre.astype(BF16)
    low = (pre - high.astype(F32)).astype(BF16)
    return high, low


def link_kernel(arrived_ref, row_ref, col_ref, w_ref, cot_ref, back_ref, arrived_s, sem):
    slots = back_ref.shape[0]
    tile = 256
    arrival = pltpu.make_async_copy(arrived_ref, arrived_s, sem)
    arrival.start()
    arrival.wait()
    for i in range(0, slots, tile):
        at = slice(i, i + tile)
        same = jnp.where(col_ref[at, :] == row_ref[...], 1.0, 0.0).astype(BF16)
        agg = mm(same, arrived_s[...]).astype(BF16)
        high, low = turn_back(agg, w_ref[...], cot_ref[at, :])
        back_ref[at, :] = (mm_t(high, w_ref[...]) + mm_t(low, w_ref[...])).astype(BF16)


def link_grad_kernel(arrived_ref, row_ref, w_ref, cot_ref, out_ref):
    tile = 256
    total = None
    for i in range(0, cot_ref.shape[0], tile):
        at = slice(i, i + tile)
        agg = mm(hot_cols(row_ref[...], i, tile), arrived_ref[...]).astype(BF16)
        high, low = turn_back(agg, w_ref[...], cot_ref[at, :])
        term = t_mm(agg, high) + t_mm(agg, low)
        total = term if total is None else total + term
    out_ref[...] = total


def backward_kernel(
    core_ref, table_ref, row_ref, cot_ref, wi_ref, ws_ref, agg_grad_ref,
    fr_ref, fu_ref, fn_ref, fm_ref, fc_ref, xs_ref, cb_ref,
    grad_ref, da_ref, mine_ref, other_ref,
    table_s, f_s, fc_s, x_s, c_s, m_s, da_s, db_s, gi_s, gs_s, grads_s, sem, da_sem, table_sem,
):
    _, hops, paths, width = f_s.shape
    slots = table_ref.shape[0]
    tile = 256
    arrival = pltpu.make_async_copy(table_ref, table_s, table_sem)
    arrival.start()

    def loads(t):
        pairs = [(ref.at[t], f_s.at[k, t]) for k, ref in enumerate(
            (fr_ref, fu_ref, fn_ref, fm_ref))]
        pairs += [
            (fc_ref.at[t], fc_s.at[t]), (xs_ref.at[t], x_s.at[t]), (cb_ref.at[t], c_s.at[t]),
        ]
        return [
            pltpu.make_async_copy(source, target, sem.at[k, t])
            for k, (source, target) in enumerate(pairs)
        ]

    def save(t):
        return pltpu.make_async_copy(da_s.at[t], da_ref.at[t], da_sem.at[t])

    order = list(range(hops))[::-1]
    for t in order:
        for copy in loads(t):
            copy.start()

    grad_ref[...] = cot_ref[...].astype(F32)
    arrival.wait()

    for t in order:
        m_s[t] = t_mm(hot_cols(row_ref[t : t + 1, :], 0, slots), table_s[...])
    for t in order:
        for copy in loads(t):
            copy.wait()
        for i in range(0, paths, tile):
            at = slice(i, i + tile)
            d = grad_ref[at, :] + m_s[t, at, :]
            dr = (d * f_s[0, t, at, :]).astype(BF16)
            du = (d * f_s[1, t, at, :]).astype(BF16)
            da_s[t, at, :width] = dr
            da_s[t, at, width : 2 * width] = du
            da_s[t, at, 2 * width :] = (d * f_s[2, t, at, :]).astype(BF16)
            db_s[t, at, :width] = dr
            db_s[t, at, width : 2 * width] = du
            db_s[t, at, 2 * width :] = (d * f_s[3, t, at, :]).astype(BF16)
            back = mm_t(db_s[t, at, :], ws_ref[...]).astype(BF16).astype(F32)
            grad_ref[at, :] = d * fc_s[t, at, :] + back
        save(t).start()
    gi_s[...] = t_mm(flat(x_s), flat(da_s))
    gs_s[...] = t_mm(flat(c_s), flat(db_s))
    two = 2 * width
    grads_s[:width, :] = gi_s[:, :two]
    grads_s[width:two, :] = gs_s[:, :two]
    grads_s[two : 3 * width, :width] = gi_s[:, two:]
    grads_s[two : 3 * width, width:] = gs_s[:, two:]
    grads_s[3 * width :, :width] = agg_grad_ref[...]
    grads_s[3 * width :, width:] = jnp.zeros_like(agg_grad_ref)
    core = core_ref[0]
    mine_ref[...] = grads_s[half_of(core, two), :]
    other_ref[...] = grads_s[half_of(1 - core, two), :].astype(BF16)
    for t in order:
        save(t).wait()


def half_of(core, lines):
    return pl.ds(pl.multiple_of(core * lines, lines), lines)


def flat(ref):
    hops, paths, width = ref.shape
    return ref[...].reshape(hops * paths, width)


def input_kernel(groups, core_ref, da_ref, row_ref, wi_ref, mine_ref, other_ref, dx_s, sums_s):
    hops, paths, _ = da_ref.shape
    for t in range(hops):
        dx_s[t * paths : (t + 1) * paths, :] = mm_t(da_ref[t], wi_ref[...]).astype(BF16)
    add_up(row_ref, dx_s, sums_s)
    run = mine_ref.shape[0] // groups
    core = core_ref[0]
    for g in range(groups):
        at = slice(g * run, (g + 1) * run)
        mine_ref[at, :] = sums_s[pl.ds(pl.multiple_of((2 * g + core) * run, run), run), :]
        other_ref[at, :] = sums_s[pl.ds(pl.multiple_of((2 * g + 1 - core) * run, run), run), :]


def share_kernel(chips, parts_ref, mine_ref, pair_ref, out_ref):
    rows, wide = parts_ref.shape
    width = mine_ref.shape[1]
    lines = rows // chips
    total = jnp.sum(parts_ref[...].reshape(chips // 2, 2 * lines, wide).astype(F32), axis=0)
    total = total[:lines] + total[lines:]
    both = jnp.concatenate([total, total], axis=0).astype(BF16)
    out_ref[:, :width] = mine_ref[...]
    out_ref[:, width : 2 * width] = pair_ref[...]
    out_ref[:, 2 * width :] = jnp.broadcast_to(
        both[None], (chips // 2, 2 * lines, wide)
    ).reshape(rows, wide)


def link_out_kernel(got_ref, mine_ref, pair_ref, cot_ref, link_ref, got_s, out_s, sem, out_sem):
    links, width = cot_ref.shape
    tile = 512
    arrival = pltpu.make_async_copy(got_ref, got_s, sem)
    arrival.start()
    arrival.wait()

    def save(k):
        at = pl.ds(k * tile, tile)
        return pltpu.make_async_copy(out_s.at[at, :], link_ref.at[at, :], out_sem.at[k])

    for k in range(links // tile):
        at = slice(k * tile, (k + 1) * tile)
        total = mm(hot_cols(mine_ref[...], k * tile, tile), got_s[:, :width])
        total += mm(hot_cols(pair_ref[...], k * tile, tile), got_s[:, width : 2 * width])
        out_s[at, :] = cot_ref[at, :].astype(F32) + total
        save(k).start()
    for k in range(links // tile):
        save(k).wait()


def grads_kernel(
    path_scale, link_scale, core_ref, mine_ref, other_ref, gi_ref, gs_ref, ga_ref, all_s,
):
    width = ga_ref.shape[0]
    two = 2 * width
    core = core_ref[0]
    all_s[half_of(core, two), :] = mine_ref[...].astype(F32)
    all_s[half_of(1 - core, two), :] = other_ref[...].astype(F32)
    gi_ref[:, :two] = all_s[:width, :] * path_scale
    gs_ref[:, :two] = all_s[width:two, :] * path_scale
    gi_ref[:, two:] = all_s[two : 3 * width, :width] * path_scale
    gs_ref[:, two:] = all_s[two : 3 * width, width:] * path_scale
    ga_ref[...] = all_s[3 * width :, :width] * link_scale


def to_pair(rows):
    return lax.ppermute(rows, "core", [(0, 1), (1, 0)])


def exchange(rows, devices, axes=AXES):
    lines, width = rows.shape
    chunks = rows.reshape(devices, lines // devices, width)
    got = lax.all_to_all(chunks, axes, split_axis=0, concat_axis=0, tiled=True)
    return got.reshape(lines, width)


def per_device(
    path_state, link_state, hop_slot, hop_count, send_rows,
    w_input, w_state, w_agg, path_cot, link_cot,
):
    groups = lax.axis_size("group")
    chips = groups * lax.axis_size("sw")
    devices = 2 * chips
    core = lax.axis_index("core")
    core_at = core.astype(jnp.int32).reshape(1)
    paths, width = path_state.shape
    hops = hop_slot.shape[1]
    links = link_state.shape[0]
    slots = devices * send_rows.shape[1]
    gate_cols = w_input.shape[1]
    shape = jax.ShapeDtypeStruct

    slot_rows = shape((slots, width), BF16)
    rows, send_row = call(
        pick_kernel, (slot_rows, shape((1, slots), jnp.int32)), [],
        (2 * slots * links * width, 2 * links * width, 16), send_rows.T, link_state,
    )
    table = exchange(rows, devices)

    valid = jnp.arange(hops, dtype=jnp.int32)[:, None] < hop_count[None, :]
    slot_row = jnp.where(valid, hop_slot.T, -1)
    count = hop_count[:, None]
    send_col = send_rows.reshape(slots, 1)
    cot_rows = call(
        pick_again_kernel, slot_rows, [],
        (2 * slots * links * width, 2 * links * width, 16), send_row, link_cot,
    )
    table, cot_rows, send_col, count, slot_row = lax.optimization_barrier(
        (table, cot_rows, send_col, count, slot_row)
    )
    sums, xs, cs = call(
        forward_kernel,
        (slot_rows, shape((hops, paths, width), BF16), shape((hops, paths, width), F32)),
        [
            pltpu.VMEM((slots, width), BF16),
            pltpu.VMEM((width, gate_cols), BF16),
            pltpu.VMEM((width, gate_cols), BF16),
            pltpu.VMEM((hops, paths, gate_cols), F32),
            pltpu.VMEM((hops, paths, width), BF16),
            pltpu.VMEM((hops, paths, width), F32),
            pltpu.VMEM((hops * paths, width), BF16),
            pltpu.SemaphoreType.DMA((2, hops)),
            pltpu.SemaphoreType.DMA,
        ],
        (4 * hops * paths * slots * width, 8 * hops * paths * width, 58),
        table, count, slot_row, path_state, w_input, w_state,
        in_specs=[ANY] + [VMEM] * 5,
        out_specs=(VMEM, ANY, ANY),
    )
    arrived = exchange(sums, devices)

    whole = lambda *dims: pl.BlockSpec(dims, lambda i: (0,) * len(dims))
    factor = shape((hops, paths, width), F32)
    short = shape((hops, paths, width), BF16)
    hop_block = pl.BlockSpec((1, paths, width), lambda i: (i, 0, 0))
    factors = pl.pallas_call(
        factors_kernel,
        grid=(hops,),
        out_shape=(short,) * 4 + (factor, short),
        in_specs=[
            hop_block, hop_block, whole(paths, 1),
            whole(width, gate_cols), whole(width, gate_cols),
        ],
        out_specs=(hop_block,) * 6,
        scratch_shapes=[pltpu.VMEM((width, gate_cols), BF16)] * 2,
        compiler_params=pltpu.CompilerParams(vmem_limit_bytes=58 * MIB),
        cost_estimate=pl.CostEstimate(
            flops=4 * hops * paths * width * gate_cols,
            bytes_accessed=32 * hops * paths * width, transcendentals=0,
        ),
    )(xs, cs, count, w_input, w_state)
    arrived, factors = lax.optimization_barrier((arrived, factors))

    back = call(
        link_kernel, slot_rows,
        [pltpu.VMEM((slots, width), BF16), pltpu.SemaphoreType.DMA],
        (2 * slots * slots * width, 8 * slots * width, 16),
        arrived, send_row, send_col, w_agg, cot_rows,
        in_specs=[ANY] + [VMEM] * 4,
    )
    back_table = exchange(back, devices)
    agg_grad = call(
        link_grad_kernel, shape((width, width), F32), [],
        (4 * links * width * width, 6 * links * width, 16), arrived, send_row, w_agg, link_cot,
    )
    back_table, agg_grad = lax.optimization_barrier((back_table, agg_grad))

    grad_path, da, mine, other = call(
        backward_kernel,
        (
            shape((paths, width), F32),
            shape((hops, paths, gate_cols), BF16),
            shape((2 * width, 2 * width), F32),
            shape((2 * width, 2 * width), BF16),
        ),
        [
            pltpu.VMEM((slots, width), BF16),
            pltpu.VMEM((4, hops, paths, width), BF16),
            pltpu.VMEM((hops, paths, width), F32),
            pltpu.VMEM((hops, paths, width), BF16),
            pltpu.VMEM((hops, paths, width), BF16),
            pltpu.VMEM((hops, paths, width), F32),
            pltpu.VMEM((hops, paths, gate_cols), BF16),
            pltpu.VMEM((hops, paths, gate_cols), BF16),
            pltpu.VMEM((width, gate_cols), F32),
            pltpu.VMEM((width, gate_cols), F32),
            pltpu.VMEM((4 * width, 2 * width), F32),
            pltpu.SemaphoreType.DMA((7, hops)),
            pltpu.SemaphoreType.DMA((hops,)),
            pltpu.SemaphoreType.DMA,
        ],
        (10 * hops * paths * width * gate_cols, 32 * hops * paths * width, 52),
        core_at, back_table, slot_row, path_cot, w_input, w_state, agg_grad,
        *factors[:5], xs, factors[5],
        in_specs=[SMEM, ANY] + [VMEM] * 5 + [ANY] * 7,
        out_specs=(VMEM, ANY, VMEM, VMEM),
    )
    added = (mine + to_pair(other).astype(F32)).astype(BF16)
    parts = exchange(added, chips, CHIPS)
    half = shape((slots // 2, width), BF16)
    my_sums, pair_sums = call(
        functools.partial(input_kernel, groups), (half, half),
        [pltpu.VMEM((hops * paths, width), BF16), pltpu.VMEM((slots, width), BF16)],
        (2 * hops * paths * (gate_cols + slots) * width, 2 * hops * paths * gate_cols, 24),
        core_at, da, slot_row, w_input,
        in_specs=[SMEM] + [VMEM] * 3,
    )
    got_sums = to_pair(pair_sums)
    lists = send_rows.reshape(groups, 2, slots // (2 * groups))
    my_list = lax.dynamic_index_in_dim(lists, core, 1, keepdims=False).reshape(1, slots // 2)
    pair_list = lax.dynamic_index_in_dim(lists, 1 - core, 1, keepdims=False).reshape(1, slots // 2)
    parts, my_sums, got_sums, my_list, pair_list = lax.optimization_barrier(
        (parts, my_sums, got_sums, my_list, pair_list)
    )
    last = call(
        functools.partial(share_kernel, chips), shape((slots // 2, 4 * width), BF16), [],
        (slots * width, 10 * slots * width, 16), parts, my_sums, got_sums,
    )
    got = exchange(last, chips, CHIPS)
    my_half = got[:, 2 * width :]
    other_half = to_pair(my_half)
    grad_link = call(
        link_out_kernel, shape((links, width), F32),
        [
            pltpu.VMEM((slots // 2, 4 * width), BF16),
            pltpu.VMEM((links, width), F32),
            pltpu.SemaphoreType.DMA,
            pltpu.SemaphoreType.DMA((links // 512,)),
        ],
        (2 * slots * links * width, 8 * links * width, 16),
        got, my_list, pair_list, link_cot,
        in_specs=[ANY] + [VMEM] * 3,
        out_specs=ANY,
    )
    wide = shape((width, gate_cols), F32)
    input_grad, state_grad, agg_total = call(
        functools.partial(
            grads_kernel, 1.0 / math.sqrt(paths * devices), 1.0 / math.sqrt(links * devices)
        ),
        (wide, wide, shape((width, width), F32)), [pltpu.VMEM((4 * width, 2 * width), F32)],
        (8 * width * width, 40 * width * width, 16), core_at, my_half, other_half,
        in_specs=[SMEM, VMEM, VMEM],
    )
    return grad_path, grad_link, input_grad, state_grad, agg_total


def solution(mesh):
    outer, sw = mesh.devices.shape
    by_core = Mesh(mesh.devices.reshape(outer // 2, 2, sw), AXES)
    split = P(AXES, None)
    return jax.shard_map(
        per_device,
        mesh=by_core,
        in_specs=(split, split, split, P(AXES), split, P(), P(), P(), split, split),
        out_specs=(split, split, P(), P(), P()),
        check_vma=False,
    )
```

```python
import functools
import math

import jax
import jax.numpy as jnp
from jax import lax
from jax.experimental import pallas as pl
from jax.experimental.pallas import tpu as pltpu
from jax.sharding import Mesh
from jax.sharding import PartitionSpec as P

F32 = jnp.float32
BF16 = jnp.bfloat16
AXES = ("group", "core", "sw")
CHIPS = ("group", "sw")
MIB = 1024 * 1024
VMEM = pl.BlockSpec(memory_space=pltpu.VMEM)
ANY = pl.BlockSpec(memory_space=pl.ANY)
SMEM = pl.BlockSpec(memory_space=pltpu.SMEM)


def mm(a, b):
    return lax.dot_general(a, b, (((1,), (0,)), ((), ())), preferred_element_type=F32)


def mm_t(a, b):
    return lax.dot_general(a, b, (((1,), (1,)), ((), ())), preferred_element_type=F32)


def t_mm(a, b):
    return lax.dot_general(a, b, (((0,), (0,)), ((), ())), preferred_element_type=F32)


def hot_cols(row, start, height):
    lines = lax.broadcasted_iota(jnp.int32, (height, row.shape[1]), 0) + start
    return jnp.where(row == lines, 1.0, 0.0).astype(BF16)


def call(kernel, outs, scratch, cost, *args, in_specs=None, out_specs=None):
    flops, moved, room = cost
    return pl.pallas_call(
        kernel,
        out_shape=outs,
        in_specs=in_specs or [VMEM] * len(args),
        out_specs=out_specs or jax.tree.map(lambda _: VMEM, outs),
        scratch_shapes=scratch,
        compiler_params=pltpu.CompilerParams(vmem_limit_bytes=room * MIB),
        cost_estimate=pl.CostEstimate(flops=flops, bytes_accessed=moved, transcendentals=0),
    )(*args)


def pick_kernel(turned_ref, link_ref, out_ref, row_ref):
    capacity, devices = turned_ref.shape
    slots = capacity * devices
    links = link_ref.shape[0]
    listed = turned_ref[...]
    high = (listed >> 8).astype(F32).astype(BF16)
    low = (listed & 255).astype(F32).astype(BF16)
    owner = lax.broadcasted_iota(jnp.int32, (devices, slots), 0)
    place = lax.broadcasted_iota(jnp.int32, (devices, slots), 1)
    spread = jnp.where(place // capacity == owner, 1.0, 0.0).astype(BF16)
    wide = mm(high, spread) * 256.0 + mm(low, spread)
    line = lax.broadcasted_iota(jnp.int32, (capacity, slots), 0)
    at = lax.broadcasted_iota(jnp.int32, (capacity, slots), 1)
    row = jnp.sum(jnp.where(at % capacity == line, wide, 0.0), axis=0, keepdims=True)
    row_ref[...] = row.astype(jnp.int32)
    step = 512
    total = None
    for i in range(0, links, step):
        term = t_mm(hot_cols(row_ref[...], i, step), link_ref[i : i + step, :])
        total = term if total is None else total + term
    out_ref[...] = total.astype(BF16)


def pick_again_kernel(row_ref, link_ref, out_ref):
    step = 512
    total = None
    for i in range(0, link_ref.shape[0], step):
        term = t_mm(hot_cols(row_ref[...], i, step), link_ref[i : i + step, :])
        total = term if total is None else total + term
    out_ref[...] = total.astype(BF16)


def halved(w_ref):
    width = w_ref.shape[0]
    lanes = lax.broadcasted_iota(jnp.int32, w_ref.shape, 1)
    w = w_ref[...].astype(F32)
    return jnp.where(lanes < 2 * width, 0.5 * w, w).astype(BF16)


def gates(a, b, width):
    r = 0.5 * jnp.tanh(a[:, :width] + b[:, :width]) + 0.5
    u = 0.5 * jnp.tanh(a[:, width : 2 * width] + b[:, width : 2 * width]) + 0.5
    bn = b[:, 2 * width :]
    n = jnp.tanh(a[:, 2 * width :] + r * bn)
    return r, u, n, bn


def forward_kernel(
    table_ref, count_ref, row_ref, start_ref, wi_ref, ws_ref,
    sums_ref, xs_ref, cs_ref, table_s, wi_s, ws_s, a_s, x_s, c_s, msg_s, sem, table_sem,
):
    hops, paths, width = x_s.shape
    slots = table_ref.shape[0]
    tile = 256
    arrival = pltpu.make_async_copy(table_ref, table_s, table_sem)
    arrival.start()
    wi_s[...] = halved(wi_ref)
    ws_s[...] = halved(ws_ref)
    c_s[0] = start_ref[...].astype(F32)
    arrival.wait()

    def saves(t):
        return (
            pltpu.make_async_copy(x_s.at[t], xs_ref.at[t], sem.at[0, t]),
            pltpu.make_async_copy(c_s.at[t], cs_ref.at[t], sem.at[1, t]),
        )

    for t in range(hops):
        hot = hot_cols(row_ref[t : t + 1, :], 0, slots)
        x_s[t] = t_mm(hot, table_s[...]).astype(BF16)

    a_s[0] = mm(x_s[0], wi_s[...])
    for t in range(hops):
        if t + 1 < hops:
            a_s[t + 1] = mm(x_s[t + 1], wi_s[...])
        for i in range(0, paths, tile):
            at = slice(i, i + tile)
            c = c_s[t, at, :]
            b = mm(c.astype(BF16), ws_s[...])
            r, u, n, _ = gates(a_s[t, at, :], b, width)
            c = jnp.where(count_ref[at, :] > t, n + u * (c - n), c)
            if t + 1 < hops:
                c_s[t + 1, at, :] = c
            msg_s[t * paths + i : t * paths + i + tile, :] = c.astype(BF16)
    for t in range(hops):
        for copy in saves(t):
            copy.start()

    add_up(row_ref, msg_s, sums_ref)
    for t in range(hops):
        for copy in saves(t):
            copy.wait()


def add_up(row_ref, values, sums_ref):
    hops, paths = row_ref.shape
    step = 256
    for i in range(0, sums_ref.shape[0], step):
        total = None
        for t in range(hops):
            hot = hot_cols(row_ref[t : t + 1, :], i, step)
            term = mm(hot, values[t * paths : (t + 1) * paths, :])
            total = term if total is None else total + term
        sums_ref[i : i + step, :] = total.astype(BF16)


def factors_kernel(
    xs_ref, cs_ref, count_ref, wi_ref, ws_ref,
    fr_ref, fu_ref, fn_ref, fm_ref, fc_ref, cb_ref, wi_s, ws_s,
):
    t = pl.program_id(0)
    _, paths, width = xs_ref.shape
    tile = 256

    @pl.when(t == 0)
    def _():
        wi_s[...] = halved(wi_ref)
        ws_s[...] = halved(ws_ref)

    for i in range(0, paths, tile):
        at = slice(i, i + tile)
        c = cs_ref[0, at, :]
        cb = c.astype(BF16)
        cb_ref[0, at, :] = cb
        r, u, n, bn = gates(mm(xs_ref[0, at, :], wi_s[...]), mm(cb, ws_s[...]), width)
        keep = count_ref[at, :] > t
        fn = jnp.where(keep, (1.0 - u) * (1.0 - n * n), 0.0)
        fm = fn * r
        fn_ref[0, at, :] = fn.astype(BF16)
        fm_ref[0, at, :] = fm.astype(BF16)
        fr_ref[0, at, :] = (fm * bn * (1.0 - r)).astype(BF16)
        fu_ref[0, at, :] = jnp.where(keep, (c - n) * u * (1.0 - u), 0.0).astype(BF16)
        fc_ref[0, at, :] = jnp.where(keep, u, 1.0)


def turn_back(agg, w, cot):
    act = jnp.tanh(mm(agg, w))
    pre = cot.astype(F32) * (1.0 - act * act)
    high = pre.astype(BF16)
    low = (pre - high.astype(F32)).astype(BF16)
    return high, low


def link_kernel(arrived_ref, row_ref, col_ref, w_ref, cot_ref, back_ref, arrived_s, sem):
    slots = back_ref.shape[0]
    tile = 256
    arrival = pltpu.make_async_copy(arrived_ref, arrived_s, sem)
    arrival.start()
    arrival.wait()
    for i in range(0, slots, tile):
        at = slice(i, i + tile)
        same = jnp.where(col_ref[at, :] == row_ref[...], 1.0, 0.0).astype(BF16)
        agg = mm(same, arrived_s[...]).astype(BF16)
        high, low = turn_back(agg, w_ref[...], cot_ref[at, :])
        back_ref[at, :] = (mm_t(high, w_ref[...]) + mm_t(low, w_ref[...])).astype(BF16)


def link_grad_kernel(arrived_ref, row_ref, w_ref, cot_ref, out_ref):
    tile = 256
    total = None
    for i in range(0, cot_ref.shape[0], tile):
        at = slice(i, i + tile)
        agg = mm(hot_cols(row_ref[...], i, tile), arrived_ref[...]).astype(BF16)
        high, low = turn_back(agg, w_ref[...], cot_ref[at, :])
        term = t_mm(agg, high) + t_mm(agg, low)
        total = term if total is None else total + term
    out_ref[...] = total


def backward_kernel(
    core_ref, table_ref, row_ref, cot_ref, turned_ref, agg_grad_ref,
    fr_ref, fu_ref, fn_ref, fm_ref, fc_ref, xs_ref, cb_ref,
    grad_ref, da_ref, mine_ref, other_ref,
    table_s, f_s, fc_s, x_s, c_s, m_s, da_s, db_s, grads_s, sem, da_sem, table_sem,
):
    _, hops, paths, width = f_s.shape
    slots = table_ref.shape[0]
    tile = 256
    arrival = pltpu.make_async_copy(table_ref, table_s, table_sem)
    arrival.start()

    def loads(t):
        pairs = [(ref.at[t], f_s.at[k, t]) for k, ref in enumerate(
            (fr_ref, fu_ref, fn_ref, fm_ref))]
        pairs += [
            (fc_ref.at[t], fc_s.at[t]), (xs_ref.at[t], x_s.at[t]), (cb_ref.at[t], c_s.at[t]),
        ]
        return [
            pltpu.make_async_copy(source, target, sem.at[k, t])
            for k, (source, target) in enumerate(pairs)
        ]

    def save(t):
        return pltpu.make_async_copy(da_s.at[t], da_ref.at[t], da_sem.at[t])

    order = list(range(hops))[::-1]
    for t in order:
        for copy in loads(t):
            copy.start()

    grad_ref[...] = cot_ref[...].astype(F32)
    arrival.wait()

    for t in order:
        m_s[t] = t_mm(hot_cols(row_ref[t : t + 1, :], 0, slots), table_s[...])
    for t in order:
        for copy in loads(t):
            copy.wait()
        for i in range(0, paths, tile):
            at = slice(i, i + tile)
            d = grad_ref[at, :] + m_s[t, at, :]
            dr = (d * f_s[0, t, at, :]).astype(BF16)
            du = (d * f_s[1, t, at, :]).astype(BF16)
            da_s[t, at, :width] = dr
            da_s[t, at, width : 2 * width] = du
            da_s[t, at, 2 * width :] = (d * f_s[2, t, at, :]).astype(BF16)
            db_s[t, at, :width] = dr
            db_s[t, at, width : 2 * width] = du
            db_s[t, at, 2 * width :] = (d * f_s[3, t, at, :]).astype(BF16)
            back = mm(db_s[t, at, :], turned_ref[...]).astype(BF16).astype(F32)
            grad_ref[at, :] = d * fc_s[t, at, :] + back
        save(t).start()
    two = 2 * width
    for k, (left, right) in enumerate(((x_s, da_s), (c_s, db_s))):
        grad = t_mm(flat(left), flat(right)).astype(BF16)
        grads_s[k * width : (k + 1) * width, :] = grad[:, :two]
        grads_s[two : 3 * width, k * width : (k + 1) * width] = grad[:, two:]
    grads_s[3 * width :, :width] = agg_grad_ref[...].astype(BF16)
    grads_s[3 * width :, width:] = jnp.zeros_like(agg_grad_ref).astype(BF16)
    core = core_ref[0]
    mine_ref[...] = grads_s[half_of(core, two), :]
    other_ref[...] = grads_s[half_of(1 - core, two), :]
    for t in order:
        save(t).wait()


def half_of(core, lines):
    return pl.ds(pl.multiple_of(core * lines, lines), lines)


def flat(ref):
    hops, paths, width = ref.shape
    return ref[...].reshape(hops * paths, width)


def input_kernel(groups, core_ref, da_ref, row_ref, turned_ref, mine_ref, other_ref, dx_s, sums_s):
    hops, paths, _ = da_ref.shape
    for t in range(hops):
        dx_s[t * paths : (t + 1) * paths, :] = mm(da_ref[t], turned_ref[...]).astype(BF16)
    add_up(row_ref, dx_s, sums_s)
    run = mine_ref.shape[0] // groups
    core = core_ref[0]
    for g in range(groups):
        at = slice(g * run, (g + 1) * run)
        mine_ref[at, :] = sums_s[pl.ds(pl.multiple_of((2 * g + core) * run, run), run), :]
        other_ref[at, :] = sums_s[pl.ds(pl.multiple_of((2 * g + 1 - core) * run, run), run), :]


def pair_kernel(mine_ref, other_ref, out_ref):
    out_ref[...] = (mine_ref[...].astype(F32) + other_ref[...].astype(F32)).astype(BF16)


def share_kernel(chips, parts_ref, mine_ref, pair_ref, out_ref):
    rows, wide = parts_ref.shape
    width = mine_ref.shape[1]
    lines = rows // chips
    total = jnp.sum(parts_ref[...].reshape(chips // 2, 2 * lines, wide).astype(F32), axis=0)
    total = total[:lines] + total[lines:]
    both = jnp.concatenate([total, total], axis=0).astype(BF16)
    out_ref[:, :width] = mine_ref[...]
    out_ref[:, width : 2 * width] = pair_ref[...]
    out_ref[:, 2 * width :] = jnp.broadcast_to(
        both[None], (chips // 2, 2 * lines, wide)
    ).reshape(rows, wide)


def link_out_kernel(got_ref, mine_ref, pair_ref, cot_ref, link_ref, got_s, out_s, sem, out_sem):
    links, width = cot_ref.shape
    tile = 512
    arrival = pltpu.make_async_copy(got_ref, got_s, sem)
    arrival.start()
    arrival.wait()

    def save(k):
        at = pl.ds(k * tile, tile)
        return pltpu.make_async_copy(out_s.at[at, :], link_ref.at[at, :], out_sem.at[k])

    for k in range(links // tile):
        at = slice(k * tile, (k + 1) * tile)
        total = mm(hot_cols(mine_ref[...], k * tile, tile), got_s[:, :width])
        total += mm(hot_cols(pair_ref[...], k * tile, tile), got_s[:, width : 2 * width])
        out_s[at, :] = cot_ref[at, :].astype(F32) + total
        save(k).start()
    for k in range(links // tile):
        save(k).wait()


def grads_kernel(
    path_scale, link_scale, core_ref, mine_ref, other_ref, gi_ref, gs_ref, ga_ref, all_s,
):
    width = ga_ref.shape[0]
    two = 2 * width
    core = core_ref[0]
    all_s[half_of(core, two), :] = mine_ref[...].astype(F32)
    all_s[half_of(1 - core, two), :] = other_ref[...].astype(F32)
    gi_ref[:, :two] = all_s[:width, :] * path_scale
    gs_ref[:, :two] = all_s[width:two, :] * path_scale
    gi_ref[:, two:] = all_s[two : 3 * width, :width] * path_scale
    gs_ref[:, two:] = all_s[two : 3 * width, width:] * path_scale
    ga_ref[...] = all_s[3 * width :, :width] * link_scale


def to_pair(rows):
    return lax.ppermute(rows, "core", [(0, 1), (1, 0)])


def exchange(rows, devices, axes=AXES):
    lines, width = rows.shape
    chunks = rows.reshape(devices, lines // devices, width)
    got = lax.all_to_all(chunks, axes, split_axis=0, concat_axis=0, tiled=True)
    return got.reshape(lines, width)


def per_device(
    path_state, link_state, hop_slot, hop_count, send_rows,
    w_input, w_state, w_agg, path_cot, link_cot,
):
    groups = lax.axis_size("group")
    chips = groups * lax.axis_size("sw")
    devices = 2 * chips
    core = lax.axis_index("core")
    core_at = core.astype(jnp.int32).reshape(1)
    paths, width = path_state.shape
    hops = hop_slot.shape[1]
    links = link_state.shape[0]
    slots = devices * send_rows.shape[1]
    gate_cols = w_input.shape[1]
    shape = jax.ShapeDtypeStruct

    slot_rows = shape((slots, width), BF16)
    rows, send_row = call(
        pick_kernel, (slot_rows, shape((1, slots), jnp.int32)), [],
        (2 * slots * links * width, 2 * links * width, 16), send_rows.T, link_state,
    )
    table = exchange(rows, devices)

    valid = jnp.arange(hops, dtype=jnp.int32)[:, None] < hop_count[None, :]
    slot_row = jnp.where(valid, hop_slot.T, -1)
    count = hop_count[:, None]
    send_col = send_rows.reshape(slots, 1)
    cot_rows = call(
        pick_again_kernel, slot_rows, [],
        (2 * slots * links * width, 2 * links * width, 16), send_row, link_cot,
    )
    input_turned = w_input.T
    state_turned = w_state.T
    table, cot_rows, send_col, count, slot_row, input_turned, state_turned = (
        lax.optimization_barrier(
            (table, cot_rows, send_col, count, slot_row, input_turned, state_turned)
        )
    )
    sums, xs, cs = call(
        forward_kernel,
        (slot_rows, shape((hops, paths, width), BF16), shape((hops, paths, width), F32)),
        [
            pltpu.VMEM((slots, width), BF16),
            pltpu.VMEM((width, gate_cols), BF16),
            pltpu.VMEM((width, gate_cols), BF16),
            pltpu.VMEM((hops, paths, gate_cols), F32),
            pltpu.VMEM((hops, paths, width), BF16),
            pltpu.VMEM((hops, paths, width), F32),
            pltpu.VMEM((hops * paths, width), BF16),
            pltpu.SemaphoreType.DMA((2, hops)),
            pltpu.SemaphoreType.DMA,
        ],
        (4 * hops * paths * slots * width, 8 * hops * paths * width, 58),
        table, count, slot_row, path_state, w_input, w_state,
        in_specs=[ANY] + [VMEM] * 5,
        out_specs=(VMEM, ANY, ANY),
    )
    arrived = exchange(sums, devices)

    whole = lambda *dims: pl.BlockSpec(dims, lambda i: (0,) * len(dims))
    factor = shape((hops, paths, width), F32)
    short = shape((hops, paths, width), BF16)
    hop_block = pl.BlockSpec((1, paths, width), lambda i: (i, 0, 0))
    factors = pl.pallas_call(
        factors_kernel,
        grid=(hops,),
        out_shape=(short,) * 4 + (factor, short),
        in_specs=[
            hop_block, hop_block, whole(paths, 1),
            whole(width, gate_cols), whole(width, gate_cols),
        ],
        out_specs=(hop_block,) * 6,
        scratch_shapes=[pltpu.VMEM((width, gate_cols), BF16)] * 2,
        compiler_params=pltpu.CompilerParams(vmem_limit_bytes=58 * MIB),
        cost_estimate=pl.CostEstimate(
            flops=4 * hops * paths * width * gate_cols,
            bytes_accessed=32 * hops * paths * width, transcendentals=0,
        ),
    )(xs, cs, count, w_input, w_state)
    arrived, factors = lax.optimization_barrier((arrived, factors))

    back = call(
        link_kernel, slot_rows,
        [pltpu.VMEM((slots, width), BF16), pltpu.SemaphoreType.DMA],
        (2 * slots * slots * width, 8 * slots * width, 16),
        arrived, send_row, send_col, w_agg, cot_rows,
        in_specs=[ANY] + [VMEM] * 4,
    )
    back_table = exchange(back, devices)
    agg_grad = call(
        link_grad_kernel, shape((width, width), F32), [],
        (4 * links * width * width, 6 * links * width, 58), arrived, send_row, w_agg, link_cot,
    )
    back_table, agg_grad = lax.optimization_barrier((back_table, agg_grad))

    grad_path, da, mine, other = call(
        backward_kernel,
        (
            shape((paths, width), F32),
            shape((hops, paths, gate_cols), BF16),
            shape((2 * width, 2 * width), BF16),
            shape((2 * width, 2 * width), BF16),
        ),
        [
            pltpu.VMEM((slots, width), BF16),
            pltpu.VMEM((4, hops, paths, width), BF16),
            pltpu.VMEM((hops, paths, width), F32),
            pltpu.VMEM((hops, paths, width), BF16),
            pltpu.VMEM((hops, paths, width), BF16),
            pltpu.VMEM((hops, paths, width), F32),
            pltpu.VMEM((hops, paths, gate_cols), BF16),
            pltpu.VMEM((hops, paths, gate_cols), BF16),
            pltpu.VMEM((4 * width, 2 * width), BF16),
            pltpu.SemaphoreType.DMA((7, hops)),
            pltpu.SemaphoreType.DMA((hops,)),
            pltpu.SemaphoreType.DMA,
        ],
        (10 * hops * paths * width * gate_cols, 32 * hops * paths * width, 52),
        core_at, back_table, slot_row, path_cot, state_turned, agg_grad,
        *factors[:5], xs, factors[5],
        in_specs=[SMEM, ANY] + [VMEM] * 4 + [ANY] * 7,
        out_specs=(VMEM, ANY, VMEM, VMEM),
    )
    added = call(
        pair_kernel, shape((slots // 2, 2 * width), BF16), [],
        (slots * width, 4 * slots * width, 8), mine, to_pair(other),
    )
    parts = exchange(added, chips, CHIPS)
    half = shape((slots // 2, width), BF16)
    my_sums, pair_sums = call(
        functools.partial(input_kernel, groups), (half, half),
        [pltpu.VMEM((hops * paths, width), BF16), pltpu.VMEM((slots, width), BF16)],
        (2 * hops * paths * (gate_cols + slots) * width, 2 * hops * paths * gate_cols, 24),
        core_at, da, slot_row, input_turned,
        in_specs=[SMEM] + [VMEM] * 3,
    )
    got_sums = to_pair(pair_sums)
    lists = send_rows.reshape(groups, 2, slots // (2 * groups))
    my_list = lax.dynamic_index_in_dim(lists, core, 1, keepdims=False).reshape(1, slots // 2)
    pair_list = lax.dynamic_index_in_dim(lists, 1 - core, 1, keepdims=False).reshape(1, slots // 2)
    parts, my_sums, got_sums, my_list, pair_list = lax.optimization_barrier(
        (parts, my_sums, got_sums, my_list, pair_list)
    )
    last = call(
        functools.partial(share_kernel, chips), shape((slots // 2, 4 * width), BF16), [],
        (slots * width, 10 * slots * width, 16), parts, my_sums, got_sums,
    )
    got = exchange(last, chips, CHIPS)
    my_half = got[:, 2 * width :]
    other_half = to_pair(my_half)
    grad_link = call(
        link_out_kernel, shape((links, width), F32),
        [
            pltpu.VMEM((slots // 2, 4 * width), BF16),
            pltpu.VMEM((links, width), F32),
            pltpu.SemaphoreType.DMA,
            pltpu.SemaphoreType.DMA((links // 512,)),
        ],
        (2 * slots * links * width, 8 * links * width, 16),
        got, my_list, pair_list, link_cot,
        in_specs=[ANY] + [VMEM] * 3,
        out_specs=ANY,
    )
    wide = shape((width, gate_cols), F32)
    input_grad, state_grad, agg_total = call(
        functools.partial(
            grads_kernel, 1.0 / math.sqrt(paths * devices), 1.0 / math.sqrt(links * devices)
        ),
        (wide, wide, shape((width, width), F32)), [pltpu.VMEM((4 * width, 2 * width), F32)],
        (8 * width * width, 40 * width * width, 16), core_at, my_half, other_half,
        in_specs=[SMEM, VMEM, VMEM],
    )
    return grad_path, grad_link, input_grad, state_grad, agg_total


def solution(mesh):
    outer, sw = mesh.devices.shape
    by_core = Mesh(mesh.devices.reshape(outer // 2, 2, sw), AXES)
    split = P(AXES, None)
    return jax.shard_map(
        per_device,
        mesh=by_core,
        in_specs=(split, split, split, P(AXES), split, P(), P(), P(), split, split),
        out_specs=(split, split, P(), P(), P()),
        check_vma=False,
    )
```

```python
import functools
import math

import jax
import jax.numpy as jnp
from jax import lax
from jax.experimental import pallas as pl
from jax.experimental.pallas import tpu as pltpu
from jax.sharding import Mesh
from jax.sharding import PartitionSpec as P

F32 = jnp.float32
BF16 = jnp.bfloat16
AXES = ("group", "core", "sw")
CHIPS = ("group", "sw")
MIB = 1024 * 1024
VMEM = pl.BlockSpec(memory_space=pltpu.VMEM)
ANY = pl.BlockSpec(memory_space=pl.ANY)
SMEM = pl.BlockSpec(memory_space=pltpu.SMEM)


def mm(a, b):
    return lax.dot_general(a, b, (((1,), (0,)), ((), ())), preferred_element_type=F32)


def mm_t(a, b):
    return lax.dot_general(a, b, (((1,), (1,)), ((), ())), preferred_element_type=F32)


def t_mm(a, b):
    return lax.dot_general(a, b, (((0,), (0,)), ((), ())), preferred_element_type=F32)


def hot_cols(row, start, height):
    lines = lax.broadcasted_iota(jnp.int32, (height, row.shape[1]), 0) + start
    return jnp.where(row == lines, 1.0, 0.0).astype(BF16)


def call(kernel, outs, scratch, cost, *args, in_specs=None, out_specs=None):
    flops, moved, room = cost
    return pl.pallas_call(
        kernel,
        out_shape=outs,
        in_specs=in_specs or [VMEM] * len(args),
        out_specs=out_specs or jax.tree.map(lambda _: VMEM, outs),
        scratch_shapes=scratch,
        compiler_params=pltpu.CompilerParams(vmem_limit_bytes=room * MIB),
        cost_estimate=pl.CostEstimate(flops=flops, bytes_accessed=moved, transcendentals=0),
    )(*args)


def pick_kernel(turned_ref, link_ref, out_ref, row_ref):
    capacity, devices = turned_ref.shape
    slots = capacity * devices
    links = link_ref.shape[0]
    listed = turned_ref[...]
    high = (listed >> 8).astype(F32).astype(BF16)
    low = (listed & 255).astype(F32).astype(BF16)
    owner = lax.broadcasted_iota(jnp.int32, (devices, slots), 0)
    place = lax.broadcasted_iota(jnp.int32, (devices, slots), 1)
    spread = jnp.where(place // capacity == owner, 1.0, 0.0).astype(BF16)
    wide = mm(high, spread) * 256.0 + mm(low, spread)
    line = lax.broadcasted_iota(jnp.int32, (capacity, slots), 0)
    at = lax.broadcasted_iota(jnp.int32, (capacity, slots), 1)
    row = jnp.sum(jnp.where(at % capacity == line, wide, 0.0), axis=0, keepdims=True)
    row_ref[...] = row.astype(jnp.int32)
    step = 512
    total = None
    for i in range(0, links, step):
        term = t_mm(hot_cols(row_ref[...], i, step), link_ref[i : i + step, :])
        total = term if total is None else total + term
    out_ref[...] = total.astype(BF16)


def pick_again_kernel(row_ref, link_ref, out_ref):
    step = 512
    total = None
    for i in range(0, link_ref.shape[0], step):
        term = t_mm(hot_cols(row_ref[...], i, step), link_ref[i : i + step, :])
        total = term if total is None else total + term
    out_ref[...] = total.astype(BF16)


def halved(w_ref):
    width = w_ref.shape[0]
    lanes = lax.broadcasted_iota(jnp.int32, w_ref.shape, 1)
    w = w_ref[...].astype(F32)
    return jnp.where(lanes < 2 * width, 0.5 * w, w).astype(BF16)


def gates(a, b, width):
    r = 0.5 * jnp.tanh(a[:, :width] + b[:, :width]) + 0.5
    u = 0.5 * jnp.tanh(a[:, width : 2 * width] + b[:, width : 2 * width]) + 0.5
    bn = b[:, 2 * width :]
    n = jnp.tanh(a[:, 2 * width :] + r * bn)
    return r, u, n, bn


def forward_kernel(
    table_ref, count_ref, row_ref, start_ref, wi_ref, ws_ref,
    sums_ref, xs_ref, cs_ref, table_s, wi_s, ws_s, a_s, x_s, c_s, msg_s, sem, table_sem,
):
    hops, paths, width = x_s.shape
    slots = table_ref.shape[0]
    tile = 256
    arrival = pltpu.make_async_copy(table_ref, table_s, table_sem)
    arrival.start()
    wi_s[...] = halved(wi_ref)
    ws_s[...] = halved(ws_ref)
    c_s[0] = start_ref[...].astype(F32)
    arrival.wait()

    def saves(t):
        return (
            pltpu.make_async_copy(x_s.at[t], xs_ref.at[t], sem.at[0, t]),
            pltpu.make_async_copy(c_s.at[t], cs_ref.at[t], sem.at[1, t]),
        )

    for t in range(hops):
        hot = hot_cols(row_ref[t : t + 1, :], 0, slots)
        x_s[t] = t_mm(hot, table_s[...]).astype(BF16)

    a_s[0] = mm(x_s[0], wi_s[...])
    for t in range(hops):
        if t + 1 < hops:
            a_s[t + 1] = mm(x_s[t + 1], wi_s[...])
        for i in range(0, paths, tile):
            at = slice(i, i + tile)
            c = c_s[t, at, :]
            b = mm(c.astype(BF16), ws_s[...])
            r, u, n, _ = gates(a_s[t, at, :], b, width)
            c = jnp.where(count_ref[at, :] > t, n + u * (c - n), c)
            if t + 1 < hops:
                c_s[t + 1, at, :] = c
            msg_s[t * paths + i : t * paths + i + tile, :] = c.astype(BF16)
    for t in range(hops):
        for copy in saves(t):
            copy.start()

    add_up(row_ref, msg_s, sums_ref)
    for t in range(hops):
        for copy in saves(t):
            copy.wait()


def add_up(row_ref, values, sums_ref):
    hops, paths = row_ref.shape
    step = 256
    for i in range(0, sums_ref.shape[0], step):
        total = None
        for t in range(hops):
            hot = hot_cols(row_ref[t : t + 1, :], i, step)
            term = mm(hot, values[t * paths : (t + 1) * paths, :])
            total = term if total is None else total + term
        sums_ref[i : i + step, :] = total.astype(BF16)


def factors_kernel(
    xs_ref, cs_ref, count_ref, wi_ref, ws_ref,
    fr_ref, fu_ref, fn_ref, fm_ref, fc_ref, cb_ref, wi_s, ws_s,
):
    t = pl.program_id(0)
    _, paths, width = xs_ref.shape
    tile = 256

    @pl.when(t == 0)
    def _():
        wi_s[...] = halved(wi_ref)
        ws_s[...] = halved(ws_ref)

    for i in range(0, paths, tile):
        at = slice(i, i + tile)
        c = cs_ref[0, at, :]
        cb = c.astype(BF16)
        cb_ref[0, at, :] = cb
        r, u, n, bn = gates(mm(xs_ref[0, at, :], wi_s[...]), mm(cb, ws_s[...]), width)
        keep = count_ref[at, :] > t
        fn = jnp.where(keep, (1.0 - u) * (1.0 - n * n), 0.0)
        fm = fn * r
        fn_ref[0, at, :] = fn.astype(BF16)
        fm_ref[0, at, :] = fm.astype(BF16)
        fr_ref[0, at, :] = (fm * bn * (1.0 - r)).astype(BF16)
        fu_ref[0, at, :] = jnp.where(keep, (c - n) * u * (1.0 - u), 0.0).astype(BF16)
        fc_ref[0, at, :] = jnp.where(keep, u, 1.0)


def turn_back(agg, w, cot):
    act = jnp.tanh(mm(agg, w))
    pre = cot.astype(F32) * (1.0 - act * act)
    high = pre.astype(BF16)
    low = (pre - high.astype(F32)).astype(BF16)
    return high, low


def link_kernel(arrived_ref, row_ref, col_ref, w_ref, cot_ref, back_ref, arrived_s, sem):
    slots = back_ref.shape[0]
    tile = 256
    arrival = pltpu.make_async_copy(arrived_ref, arrived_s, sem)
    arrival.start()
    arrival.wait()
    for i in range(0, slots, tile):
        at = slice(i, i + tile)
        same = jnp.where(col_ref[at, :] == row_ref[...], 1.0, 0.0).astype(BF16)
        agg = mm(same, arrived_s[...]).astype(BF16)
        high, low = turn_back(agg, w_ref[...], cot_ref[at, :])
        back_ref[at, :] = (mm_t(high, w_ref[...]) + mm_t(low, w_ref[...])).astype(BF16)


def link_grad_kernel(arrived_ref, row_ref, w_ref, cot_ref, out_ref):
    tile = 256
    total = None
    for i in range(0, cot_ref.shape[0], tile):
        at = slice(i, i + tile)
        agg = mm(hot_cols(row_ref[...], i, tile), arrived_ref[...]).astype(BF16)
        high, low = turn_back(agg, w_ref[...], cot_ref[at, :])
        term = t_mm(agg, high) + t_mm(agg, low)
        total = term if total is None else total + term
    out_ref[...] = total


def backward_kernel(
    table_ref, row_ref, cot_ref, wi_ref, ws_ref, agg_grad_ref,
    fr_ref, fu_ref, fn_ref, fm_ref, fc_ref, xs_ref, cb_ref,
    grad_ref, da_ref, grads_ref,
    table_s, f_s, fc_s, x_s, c_s, m_s, da_s, db_s, gi_s, gs_s, sem, da_sem, table_sem,
):
    _, hops, paths, width = f_s.shape
    slots = table_ref.shape[0]
    tile = 256
    arrival = pltpu.make_async_copy(table_ref, table_s, table_sem)
    arrival.start()

    def loads(t):
        pairs = [(ref.at[t], f_s.at[k, t]) for k, ref in enumerate(
            (fr_ref, fu_ref, fn_ref, fm_ref))]
        pairs += [
            (fc_ref.at[t], fc_s.at[t]), (xs_ref.at[t], x_s.at[t]), (cb_ref.at[t], c_s.at[t]),
        ]
        return [
            pltpu.make_async_copy(source, target, sem.at[k, t])
            for k, (source, target) in enumerate(pairs)
        ]

    def save(t):
        return pltpu.make_async_copy(da_s.at[t], da_ref.at[t], da_sem.at[t])

    order = list(range(hops))[::-1]
    for t in order:
        for copy in loads(t):
            copy.start()

    grad_ref[...] = cot_ref[...].astype(F32)
    arrival.wait()

    for t in order:
        m_s[t] = t_mm(hot_cols(row_ref[t : t + 1, :], 0, slots), table_s[...])
    for t in order:
        for copy in loads(t):
            copy.wait()
        for i in range(0, paths, tile):
            at = slice(i, i + tile)
            d = grad_ref[at, :] + m_s[t, at, :]
            dr = (d * f_s[0, t, at, :]).astype(BF16)
            du = (d * f_s[1, t, at, :]).astype(BF16)
            da_s[t, at, :width] = dr
            da_s[t, at, width : 2 * width] = du
            da_s[t, at, 2 * width :] = (d * f_s[2, t, at, :]).astype(BF16)
            db_s[t, at, :width] = dr
            db_s[t, at, width : 2 * width] = du
            db_s[t, at, 2 * width :] = (d * f_s[3, t, at, :]).astype(BF16)
            back = mm_t(db_s[t, at, :], ws_ref[...]).astype(BF16).astype(F32)
            grad_ref[at, :] = d * fc_s[t, at, :] + back
        save(t).start()
    gi_s[...] = t_mm(flat(x_s), flat(da_s))
    gs_s[...] = t_mm(flat(c_s), flat(db_s))
    two = 2 * width
    grads_ref[:width, :] = gi_s[:, :two].astype(BF16)
    grads_ref[width:two, :] = gs_s[:, :two].astype(BF16)
    grads_ref[two : 3 * width, :width] = gi_s[:, two:].astype(BF16)
    grads_ref[two : 3 * width, width:] = gs_s[:, two:].astype(BF16)
    grads_ref[3 * width :, :width] = agg_grad_ref[...].astype(BF16)
    grads_ref[3 * width :, width:] = jnp.zeros_like(agg_grad_ref).astype(BF16)
    for t in order:
        save(t).wait()


def split_kernel(core_ref, grads_ref, mine_ref, other_ref):
    half = mine_ref.shape[0]
    core = core_ref[0]
    mine_ref[...] = grads_ref[half_of(core, half), :]
    other_ref[...] = grads_ref[half_of(1 - core, half), :]


def half_of(core, lines):
    return pl.ds(pl.multiple_of(core * lines, lines), lines)


def flat(ref):
    hops, paths, width = ref.shape
    return ref[...].reshape(hops * paths, width)


def input_kernel(groups, core_ref, da_ref, row_ref, turned_ref, mine_ref, other_ref, dx_s, sums_s):
    hops, paths, _ = da_ref.shape
    for t in range(hops):
        dx_s[t * paths : (t + 1) * paths, :] = mm(da_ref[t], turned_ref[...]).astype(BF16)
    add_up(row_ref, dx_s, sums_s)
    run = mine_ref.shape[0] // groups
    core = core_ref[0]
    for g in range(groups):
        at = slice(g * run, (g + 1) * run)
        mine_ref[at, :] = sums_s[pl.ds(pl.multiple_of((2 * g + core) * run, run), run), :]
        other_ref[at, :] = sums_s[pl.ds(pl.multiple_of((2 * g + 1 - core) * run, run), run), :]


def pair_kernel(mine_ref, other_ref, out_ref):
    out_ref[...] = (mine_ref[...].astype(F32) + other_ref[...].astype(F32)).astype(BF16)


def share_kernel(chips, parts_ref, mine_ref, pair_ref, out_ref):
    rows, wide = parts_ref.shape
    width = mine_ref.shape[1]
    lines = rows // chips
    total = jnp.sum(parts_ref[...].reshape(chips // 2, 2 * lines, wide).astype(F32), axis=0)
    total = total[:lines] + total[lines:]
    both = jnp.concatenate([total, total], axis=0).astype(BF16)
    out_ref[:, :width] = mine_ref[...]
    out_ref[:, width : 2 * width] = pair_ref[...]
    out_ref[:, 2 * width :] = jnp.broadcast_to(
        both[None], (chips // 2, 2 * lines, wide)
    ).reshape(rows, wide)


def link_out_kernel(got_ref, mine_ref, pair_ref, cot_ref, link_ref, got_s, out_s, sem, out_sem):
    links, width = cot_ref.shape
    tile = 512
    arrival = pltpu.make_async_copy(got_ref, got_s, sem)
    arrival.start()
    arrival.wait()

    def save(k):
        at = pl.ds(k * tile, tile)
        return pltpu.make_async_copy(out_s.at[at, :], link_ref.at[at, :], out_sem.at[k])

    for k in range(links // tile):
        at = slice(k * tile, (k + 1) * tile)
        total = mm(hot_cols(mine_ref[...], k * tile, tile), got_s[:, :width])
        total += mm(hot_cols(pair_ref[...], k * tile, tile), got_s[:, width : 2 * width])
        out_s[at, :] = cot_ref[at, :].astype(F32) + total
        save(k).start()
    for k in range(links // tile):
        save(k).wait()


def grads_kernel(
    path_scale, link_scale, core_ref, mine_ref, other_ref, gi_ref, gs_ref, ga_ref, all_s,
):
    width = ga_ref.shape[0]
    two = 2 * width
    core = core_ref[0]
    all_s[half_of(core, two), :] = mine_ref[...].astype(F32)
    all_s[half_of(1 - core, two), :] = other_ref[...].astype(F32)
    gi_ref[:, :two] = all_s[:width, :] * path_scale
    gs_ref[:, :two] = all_s[width:two, :] * path_scale
    gi_ref[:, two:] = all_s[two : 3 * width, :width] * path_scale
    gs_ref[:, two:] = all_s[two : 3 * width, width:] * path_scale
    ga_ref[...] = all_s[3 * width :, :width] * link_scale


def to_pair(rows):
    return lax.ppermute(rows, "core", [(0, 1), (1, 0)])


def exchange(rows, devices, axes=AXES):
    lines, width = rows.shape
    chunks = rows.reshape(devices, lines // devices, width)
    got = lax.all_to_all(chunks, axes, split_axis=0, concat_axis=0, tiled=True)
    return got.reshape(lines, width)


def per_device(
    path_state, link_state, hop_slot, hop_count, send_rows,
    w_input, w_state, w_agg, path_cot, link_cot,
):
    groups = lax.axis_size("group")
    chips = groups * lax.axis_size("sw")
    devices = 2 * chips
    core = lax.axis_index("core")
    core_at = core.astype(jnp.int32).reshape(1)
    paths, width = path_state.shape
    hops = hop_slot.shape[1]
    links = link_state.shape[0]
    slots = devices * send_rows.shape[1]
    gate_cols = w_input.shape[1]
    shape = jax.ShapeDtypeStruct

    slot_rows = shape((slots, width), BF16)
    rows, send_row = call(
        pick_kernel, (slot_rows, shape((1, slots), jnp.int32)), [],
        (2 * slots * links * width, 2 * links * width, 16), send_rows.T, link_state,
    )
    table = exchange(rows, devices)

    valid = jnp.arange(hops, dtype=jnp.int32)[:, None] < hop_count[None, :]
    slot_row = jnp.where(valid, hop_slot.T, -1)
    count = hop_count[:, None]
    send_col = send_rows.reshape(slots, 1)
    cot_rows = call(
        pick_again_kernel, slot_rows, [],
        (2 * slots * links * width, 2 * links * width, 16), send_row, link_cot,
    )
    input_turned = w_input.T
    table, cot_rows, send_col, count, slot_row, input_turned = lax.optimization_barrier(
        (table, cot_rows, send_col, count, slot_row, input_turned)
    )
    sums, xs, cs = call(
        forward_kernel,
        (slot_rows, shape((hops, paths, width), BF16), shape((hops, paths, width), F32)),
        [
            pltpu.VMEM((slots, width), BF16),
            pltpu.VMEM((width, gate_cols), BF16),
            pltpu.VMEM((width, gate_cols), BF16),
            pltpu.VMEM((hops, paths, gate_cols), F32),
            pltpu.VMEM((hops, paths, width), BF16),
            pltpu.VMEM((hops, paths, width), F32),
            pltpu.VMEM((hops * paths, width), BF16),
            pltpu.SemaphoreType.DMA((2, hops)),
            pltpu.SemaphoreType.DMA,
        ],
        (4 * hops * paths * slots * width, 8 * hops * paths * width, 58),
        table, count, slot_row, path_state, w_input, w_state,
        in_specs=[ANY] + [VMEM] * 5,
        out_specs=(VMEM, ANY, ANY),
    )
    arrived = exchange(sums, devices)

    whole = lambda *dims: pl.BlockSpec(dims, lambda i: (0,) * len(dims))
    factor = shape((hops, paths, width), F32)
    short = shape((hops, paths, width), BF16)
    hop_block = pl.BlockSpec((1, paths, width), lambda i: (i, 0, 0))
    factors = pl.pallas_call(
        factors_kernel,
        grid=(hops,),
        out_shape=(short,) * 4 + (factor, short),
        in_specs=[
            hop_block, hop_block, whole(paths, 1),
            whole(width, gate_cols), whole(width, gate_cols),
        ],
        out_specs=(hop_block,) * 6,
        scratch_shapes=[pltpu.VMEM((width, gate_cols), BF16)] * 2,
        compiler_params=pltpu.CompilerParams(vmem_limit_bytes=58 * MIB),
        cost_estimate=pl.CostEstimate(
            flops=4 * hops * paths * width * gate_cols,
            bytes_accessed=32 * hops * paths * width, transcendentals=0,
        ),
    )(xs, cs, count, w_input, w_state)
    arrived, factors = lax.optimization_barrier((arrived, factors))

    back = call(
        link_kernel, slot_rows,
        [pltpu.VMEM((slots, width), BF16), pltpu.SemaphoreType.DMA],
        (2 * slots * slots * width, 8 * slots * width, 16),
        arrived, send_row, send_col, w_agg, cot_rows,
        in_specs=[ANY] + [VMEM] * 4,
    )
    back_table = exchange(back, devices)
    agg_grad = call(
        link_grad_kernel, shape((width, width), F32), [],
        (4 * links * width * width, 6 * links * width, 58), arrived, send_row, w_agg, link_cot,
    )
    back_table, agg_grad = lax.optimization_barrier((back_table, agg_grad))

    grad_path, da, grads = call(
        backward_kernel,
        (
            shape((paths, width), F32),
            shape((hops, paths, gate_cols), BF16),
            shape((4 * width, 2 * width), BF16),
        ),
        [
            pltpu.VMEM((slots, width), BF16),
            pltpu.VMEM((4, hops, paths, width), BF16),
            pltpu.VMEM((hops, paths, width), F32),
            pltpu.VMEM((hops, paths, width), BF16),
            pltpu.VMEM((hops, paths, width), BF16),
            pltpu.VMEM((hops, paths, width), F32),
            pltpu.VMEM((hops, paths, gate_cols), BF16),
            pltpu.VMEM((hops, paths, gate_cols), BF16),
            pltpu.VMEM((width, gate_cols), F32),
            pltpu.VMEM((width, gate_cols), F32),
            pltpu.SemaphoreType.DMA((7, hops)),
            pltpu.SemaphoreType.DMA((hops,)),
            pltpu.SemaphoreType.DMA,
        ],
        (10 * hops * paths * width * gate_cols, 32 * hops * paths * width, 52),
        back_table, slot_row, path_cot, w_input, w_state, agg_grad,
        *factors[:5], xs, factors[5],
        in_specs=[ANY] + [VMEM] * 5 + [ANY] * 7,
        out_specs=(VMEM, ANY, VMEM),
    )
    grad_half = shape((2 * width, 2 * width), BF16)
    mine, other = call(
        split_kernel, (grad_half, grad_half), [], (slots * width, 4 * slots * width, 8),
        core_at, grads, in_specs=[SMEM, VMEM],
    )
    added = call(
        pair_kernel, shape((slots // 2, 2 * width), BF16), [],
        (slots * width, 4 * slots * width, 8), mine, to_pair(other),
    )
    parts = exchange(added, chips, CHIPS)
    half = shape((slots // 2, width), BF16)
    my_sums, pair_sums = call(
        functools.partial(input_kernel, groups), (half, half),
        [pltpu.VMEM((hops * paths, width), BF16), pltpu.VMEM((slots, width), BF16)],
        (2 * hops * paths * (gate_cols + slots) * width, 2 * hops * paths * gate_cols, 24),
        core_at, da, slot_row, input_turned,
        in_specs=[SMEM] + [VMEM] * 3,
    )
    got_sums = to_pair(pair_sums)
    lists = send_rows.reshape(groups, 2, slots // (2 * groups))
    my_list = lax.dynamic_index_in_dim(lists, core, 1, keepdims=False).reshape(1, slots // 2)
    pair_list = lax.dynamic_index_in_dim(lists, 1 - core, 1, keepdims=False).reshape(1, slots // 2)
    parts, my_sums, got_sums, my_list, pair_list = lax.optimization_barrier(
        (parts, my_sums, got_sums, my_list, pair_list)
    )
    last = call(
        functools.partial(share_kernel, chips), shape((slots // 2, 4 * width), BF16), [],
        (slots * width, 10 * slots * width, 16), parts, my_sums, got_sums,
    )
    got = exchange(last, chips, CHIPS)
    my_half = got[:, 2 * width :]
    other_half = to_pair(my_half)
    grad_link = call(
        link_out_kernel, shape((links, width), F32),
        [
            pltpu.VMEM((slots // 2, 4 * width), BF16),
            pltpu.VMEM((links, width), F32),
            pltpu.SemaphoreType.DMA,
            pltpu.SemaphoreType.DMA((links // 512,)),
        ],
        (2 * slots * links * width, 8 * links * width, 16),
        got, my_list, pair_list, link_cot,
        in_specs=[ANY] + [VMEM] * 3,
        out_specs=ANY,
    )
    wide = shape((width, gate_cols), F32)
    input_grad, state_grad, agg_total = call(
        functools.partial(
            grads_kernel, 1.0 / math.sqrt(paths * devices), 1.0 / math.sqrt(links * devices)
        ),
        (wide, wide, shape((width, width), F32)), [pltpu.VMEM((4 * width, 2 * width), F32)],
        (8 * width * width, 40 * width * width, 16), core_at, my_half, other_half,
        in_specs=[SMEM, VMEM, VMEM],
    )
    return grad_path, grad_link, input_grad, state_grad, agg_total


def solution(mesh):
    outer, sw = mesh.devices.shape
    by_core = Mesh(mesh.devices.reshape(outer // 2, 2, sw), AXES)
    split = P(AXES, None)
    return jax.shard_map(
        per_device,
        mesh=by_core,
        in_specs=(split, split, split, P(AXES), split, P(), P(), P(), split, split),
        out_specs=(split, split, P(), P(), P()),
        check_vma=False,
    )
```
